128 devices in a mesh: role: 2 (over y_hi), dev: 64 (over z, x, y_lo, core).
Axes of the slice: x: 4, y: 4 (y_hi: 2, y_lo: 2; y = y_hi * 2 + y_lo), z: 4, core: 2. Of those that a mesh axis runs over, the one named last changes fastest.
Arguments:
- hidden: bfloat16 [1024, 7168], P(('role', 'dev')), may hold values from -6 to 6
- router: bfloat16 [7168, 32], replicated, may hold values from -0.0625 to 0.0625
- routes: int32 [1024, 8], P(('role', 'dev')), may hold values from 0 to 31, all different within a row; in each aligned block of 8 rows (0 to 7, 8 to 15, ...) at most 4 rows name the same one
- w_gate: bfloat16 [128, 7168, 256], P(('role', 'dev')), may hold values from -0.0625 to 0.0625
- w_up: bfloat16 [128, 7168, 256], P(('role', 'dev')), may hold values from -0.0625 to 0.0625
- w_down: bfloat16 [128, 256, 7168], P(('role', 'dev')), may hold values from -0.1875 to 0.1875
- w_latent: bfloat16 [7168, 576], replicated, may hold values from -0.0625 to 0.0625
- lengths: int32 [1024], P(('role', 'dev')), may hold values from 1 to 384, 196608 in all
- latent_cache: bfloat16 [1024, 384, 576], P(('role', 'dev')), may hold values from -4 to 4
- queries: bfloat16 [1024, 128, 576], P(('role', 'dev')), may hold values from -32 to 32
Outputs:
- layer_out: bfloat16 [1024, 7168], P(('role', 'dev'))
- attention: bfloat16 [1024, 128, 512], P(('role', 'dev'))
The draws below stay inside these ranges and needn't reach their ends.
Inputs may be any that keep to these rules, and one draw needn't show every extreme that they name: `routes`: in the rows of one device no expert is named by more than 4 tokens.
All inputs are finite; a program needn't handle non-finite values. No bound on the sum of `lengths` on one device may be relied on, other than what follows from the above.
Results may differ from the reference program's by a relative error of at most 0.0065.
Values may be sent and summed in bfloat16 or wider, within the bound.
No kernel may reach another device: no remote copies, remote signals or barrier semaphores. Data moves between devices by JAX's collectives and lax.ppermute only.
A program may use at most 128 MiB of HBM per device.

```python
import math
from functools import partial
import jax
import jax.numpy as jnp
import numpy as np
from jax import lax

D = 7168
FF = 1024
HEADS = 128
KVL = 512
ROPE = 64
QK_DIM = 192
TOPK = 8
R_DEV = 8
L = 384
EXPERTS = 32
CAP = 4
REQUESTS = 1024
DEVICES = 128


def cache_field(key):
    gauss_key = jax.random.fold_in(key, 0)
    shape_full = (REQUESTS, L, KVL + ROPE)
    gauss = jnp.clip(jax.random.normal(gauss_key, shape_full, jnp.float32), -4.0, 4.0)
    return gauss


def draw_latent_cache(key, part):
    field = cache_field(key)
    return field.astype(jnp.bfloat16)


def draw_queries(key, part):
    key = jax.random.fold_in(key, 12)
    shape_full = (REQUESTS, HEADS, KVL + ROPE)
    result = jnp.clip(jax.random.normal(key, shape_full, jnp.float32), -4.0, 4.0)
    return result.astype(jnp.bfloat16)


def block_scale(key, dims, shards, low, top_value):
    def one(axis_at, shards_of):
        draws = jax.random.uniform(jax.random.fold_in(jax.random.fold_in(key, 6), axis_at), (shards_of,), jnp.float32, low / len(shards), top_value / len(shards))
        return jnp.repeat(jnp.exp(draws), dims[axis_at] // shards_of).reshape((-1,) + (1,) * (len(dims) - axis_at - 1))

    factor_of = one(*shards[0])
    for cut in shards[1:]:
        factor_of = factor_of * one(*cut)
    return factor_of


def length_profile(number_of, total, reach, skew):
    portions = [(1 << 20) // math.isqrt(standing ** skew) + 1 for standing in range(2, number_of + 1)]
    spare, holding = total - reach - (number_of - 1), [1] * (number_of - 1)
    while spare > 0:
        free = [i for i in range(number_of - 1) if holding[i] < reach]
        mass, left = sum([portions[i] for i in free]), spare
        for i in free:
            addition = min(reach - holding[i], max(1, left * portions[i] // mass), spare)
            holding[i] = holding[i] + addition
            spare = spare - addition
    return np.array([reach] + holding)


def ragged(own_key, count, total, bound, lean):
    if count == 2:
        one = jax.random.randint(own_key, (), max(1, total - bound), min(bound, total - 1) + 1)
        return jnp.stack([one, total - one])
    sizes = jnp.asarray(length_profile(count, total, bound, lean), jnp.int32)
    twos = (count - 1) // 2
    source_of, sink = sizes[1:1 + 2 * twos:2], sizes[2:2 + 2 * twos:2]
    margin = jnp.minimum(source_of - 1, bound - sink)
    passed = jax.random.randint(jax.random.fold_in(own_key, 1), (twos,), 0, 1 << 20) % (margin + 1)
    sizes = sizes.at[1:1 + 2 * twos:2].set(source_of - passed).at[2:2 + 2 * twos:2].set(sink + passed)
    return sizes[jax.random.permutation(jax.random.fold_in(own_key, 2), count)]


def deal_out(stream_key, own, number, rows, amount, top, most, skew):
    sequence = jax.random.permutation(stream_key, amount)
    crowded, common = load_shares(amount, rows * top, most, skew, True), load_shares(amount, rows * top, most, skew, False)
    places = jnp.arange(amount)

    def named(tallies, rotation):
        used = int((tallies > 0).sum())
        fixed = max(1, used // 4)
        shifted = fixed + (places - fixed + rotation * (used - fixed)) % max(1, amount - fixed)
        return jnp.zeros((amount,), jnp.int32).at[sequence[jnp.where(places < fixed, places, shifted)]].set(jnp.asarray(tallies, jnp.int32))

    tallies = jnp.where(number % 4 == 0, named(crowded, number // 4), named(common, number - number // 4 - 1))
    mixed = jax.random.permutation(jax.random.fold_in(own, 3), amount)
    giver, taker = mixed[0:amount // 2 * 2:2], mixed[1:amount // 2 * 2:2]
    margin = jnp.minimum(tallies[giver] - 1, most - tallies[taker]) // 2
    margin = jnp.where((giver == sequence[0]) | (taker == sequence[0]) | (tallies[taker] == 0), 0, jnp.maximum(margin, 0))
    shifted = jax.random.randint(jax.random.fold_in(own, 4), (amount // 2,), 0, 1 << 20) % (margin + 1)
    tallies = tallies.at[giver].add(-shifted).at[taker].add(shifted)
    items = jnp.searchsorted(jnp.cumsum(tallies), jnp.arange(rows * top), side="right").astype(jnp.int32)
    listing = items.reshape(top, rows).T
    listing = listing[jax.random.permutation(jax.random.fold_in(own, 1), rows)]
    rotation = jax.random.randint(jax.random.fold_in(own, 2), (rows, 1), 0, top)
    return jnp.take_along_axis(listing, (jnp.arange(top)[None, :] + rotation) % top, axis=1)


def load_shares(count, total, most, lean, full):
    weights = [(1 << 20) // math.isqrt(rank ** lean) + 1 for rank in range(1, count + 1)]
    largest = most if full else min(most, max(-(-total // count), total * weights[0] // sum(weights)))
    least = 1 if total - largest >= count - 1 else 0
    counts, surplus = [largest] + [least] * (count - 1), total - largest - least * (count - 1)
    while surplus > 0:
        movable = [i for i in range(1, count) if counts[i] < largest] or [i for i in range(1, count) if counts[i] < most]
        pool, remaining = sum([weights[i] for i in movable]), surplus
        for i in movable:
            addition = min(most - counts[i], max(1, remaining * weights[i] // pool), surplus)
            counts[i] = counts[i] + addition
            surplus = surplus - addition
    return np.array(counts)


def scatter_about(stream_key, shape, scale, limit, shards=(), kind=jnp.bfloat16):
    level = block_scale(stream_key, shape, shards, -0.22, 0.18) if shards else 1.0
    values = jax.random.normal(stream_key, shape, jnp.float32) * scale * level
    return jnp.minimum(jnp.maximum(values, -limit), limit).astype(kind)


def setup_inputs(seed: int = 0) -> dict:
    arg_keys = jax.random.split(jax.random.key(seed), 11)
    hidden = scatter_about(arg_keys[0], (REQUESTS, D), 1.0, 6.0, ((0, 128),))
    router = scatter_about(arg_keys[1], (D, EXPERTS), D ** -0.5, 0.0625)
    routes_keys = jax.random.split(jax.random.fold_in(arg_keys[2], 1), REQUESTS // R_DEV)
    routes_turns = jax.random.permutation(jax.random.fold_in(arg_keys[2], 3), REQUESTS // R_DEV)
    routes = jax.vmap(lambda own, number: deal_out(jax.random.fold_in(arg_keys[2], 2), own, number, R_DEV, EXPERTS, TOPK, CAP, 2))(routes_keys, routes_turns).reshape((REQUESTS, TOPK))
    w_gate = scatter_about(arg_keys[3], (4 * EXPERTS, D, FF // 4), D ** -0.5, 0.0625, ((0, 128),))
    w_up = scatter_about(arg_keys[4], (4 * EXPERTS, D, FF // 4), D ** -0.5, 0.0625, ((0, 128),))
    w_down = scatter_about(arg_keys[5], (4 * EXPERTS, FF // 4, D), FF ** -0.5, 0.1875, ((0, 128),))
    w_latent = scatter_about(arg_keys[6], (D, KVL + ROPE), D ** -0.5, 0.0625)
    lengths = ragged(arg_keys[7], REQUESTS, REQUESTS * L // 2, L, 2).astype(jnp.int32)
    latent_cache = draw_latent_cache(jax.random.fold_in(arg_keys[10], 71), 0)
    queries = draw_queries(jax.random.fold_in(arg_keys[10], 71), 0)
    return dict(hidden=hidden, router=router, routes=routes, w_gate=w_gate, w_up=w_up, w_down=w_down, w_latent=w_latent, lengths=lengths, latent_cache=latent_cache, queries=queries)


def normalize(values):
    return values * lax.rsqrt(lax.optimization_barrier(jnp.mean(values * values, axis=-1, keepdims=True)) + 1e-06)

def prepare(router, experts, capacity, hidden, routes):
    normed = normalize(hidden.astype(jnp.float32)).astype(jnp.bfloat16)
    logits = jnp.dot(normed, router, preferred_element_type=jnp.float32)
    labels = jnp.arange(experts, dtype=jnp.int32)
    chosen = routes[:, :, None] == labels[None, None, :]
    picked = lax.optimization_barrier(jnp.sum(jnp.where(chosen, logits[:, None, :], 0.0), axis=2))
    affinity = jax.nn.sigmoid(picked)
    weights = 2.5 * affinity / lax.optimization_barrier(jnp.sum(affinity, axis=1, keepdims=True))
    flat_ids = routes.reshape(-1)
    member = (flat_ids[:, None] == labels[None, :]).astype(jnp.int32)
    before = jnp.cumsum(member, axis=0) - member
    slots = lax.optimization_barrier(jnp.sum(before * member, axis=1)).reshape(routes.shape)
    places = routes * capacity + slots
    cells = jnp.arange(experts * capacity, dtype=jnp.int32)
    layout = lax.optimization_barrier(jnp.sum((cells[:, None, None] == places[None, :, :]).astype(jnp.int32), axis=2)).astype(jnp.bfloat16)
    outgoing = jnp.dot(layout, normed, preferred_element_type=jnp.float32).astype(jnp.bfloat16)
    return (weights, places, outgoing.reshape(experts, capacity, normed.shape[1]))

def expert_block(token_rows, gate_slab, up_slab, down_slab):
    flat_rows = token_rows.reshape(-1, token_rows.shape[-1])
    gated = jnp.dot(flat_rows, gate_slab, preferred_element_type=jnp.float32)
    lifted = jnp.dot(flat_rows, up_slab, preferred_element_type=jnp.float32)
    inner = (jax.nn.silu(gated) * lifted).astype(jnp.bfloat16)
    return jnp.dot(inner, down_slab, preferred_element_type=jnp.float32).astype(jnp.bfloat16).reshape(token_rows.shape)

def rotate(values, positions):
    half = values.shape[-1] // 2
    indices = jnp.arange(half, dtype=jnp.float32)
    inverse = jnp.exp(indices * (-2.0 * math.log(10000.0) / values.shape[-1]))
    angles = positions.astype(jnp.float32)[:, None] * inverse[None, :]
    leading = values[:, :half]
    trailing = values[:, half:]
    return jnp.concatenate([leading * jnp.cos(angles) - trailing * jnp.sin(angles), leading * jnp.sin(angles) + trailing * jnp.cos(angles)], axis=1)

def new_entry(layer_out, w_latent, lengths):
    input_new = normalize(layer_out.astype(jnp.float32)).astype(jnp.bfloat16)
    projected = jnp.dot(input_new, w_latent, preferred_element_type=jnp.float32)
    latent_new = normalize(projected[:, :KVL]).astype(jnp.bfloat16)
    rotary_new = rotate(projected[:, KVL:], lengths).astype(jnp.bfloat16)
    return (latent_new, jnp.concatenate([latent_new, rotary_new], axis=1))

def attend(layer_out, w_latent, lengths, latent_cache, queries):
    latent_new, key_new = new_entry(layer_out, w_latent, lengths)
    scale = 1.0 / math.sqrt(QK_DIM)
    query_wide = queries.astype(jnp.float32)
    scores = jnp.einsum('rhc,rjc->rhj', query_wide, latent_cache.astype(jnp.float32)) * scale
    own = jnp.einsum('rhc,rc->rh', query_wide, key_new.astype(jnp.float32)) * scale
    positions = jnp.arange(latent_cache.shape[1], dtype=jnp.int32)
    valid = positions[None, None, :] < lengths[:, None, None]
    masked = jnp.where(valid, scores, -jnp.inf)
    highest = jnp.maximum(lax.optimization_barrier(jnp.max(masked, axis=2)), own)
    probs = jnp.where(valid, jnp.exp(masked - highest[:, :, None]), 0.0).astype(jnp.bfloat16)
    own_prob = jnp.exp(own - highest).astype(jnp.bfloat16)
    total = lax.optimization_barrier(jnp.sum(probs.astype(jnp.float32), axis=2)) + own_prob.astype(jnp.float32)
    summed = jnp.einsum('rhj,rjc->rhc', probs.astype(jnp.float32), latent_cache[:, :, :KVL].astype(jnp.float32))
    summed = summed + own_prob.astype(jnp.float32)[:, :, None] * latent_new.astype(jnp.float32)[:, None, :]
    return (summed / total[:, :, None]).astype(jnp.bfloat16)

def lookup_rows(returned, places):
    return returned[places]

def reference(hidden, router, routes, w_gate, w_up, w_down, w_latent, lengths, latent_cache, queries):
    shaped_hidden = hidden.reshape(DEVICES, R_DEV, D)
    weights, places, outgoing = jax.vmap(partial(prepare, router, EXPERTS, CAP))(shaped_hidden, routes.reshape(DEVICES, R_DEV, TOPK))
    gate_quarters = w_gate.reshape(4, EXPERTS, D, FF // 4)
    up_quarters = w_up.reshape(4, EXPERTS, D, FF // 4)
    down_quarters = w_down.reshape(4, EXPERTS, FF // 4, D)

    def serve_expert(expert):
        token_rows = lax.dynamic_index_in_dim(outgoing, expert, axis=1, keepdims=False)
        quarters = []
        for quarter in range(4):
            quarters.append(expert_block(token_rows, lax.dynamic_index_in_dim(gate_quarters[quarter], expert, 0, False), lax.dynamic_index_in_dim(up_quarters[quarter], expert, 0, False), lax.dynamic_index_in_dim(down_quarters[quarter], expert, 0, False)))
        first_pair = (quarters[0].astype(jnp.float32) + quarters[2].astype(jnp.float32)).astype(jnp.bfloat16)
        second_pair = (quarters[1].astype(jnp.float32) + quarters[3].astype(jnp.float32)).astype(jnp.bfloat16)
        return (first_pair.astype(jnp.float32) + second_pair.astype(jnp.float32)).astype(jnp.bfloat16)
    served = lax.map(serve_expert, jnp.arange(EXPERTS, dtype=jnp.int32))
    returned = jnp.moveaxis(served, 1, 0).reshape(DEVICES, EXPERTS * CAP, D)
    picked = jax.vmap(lookup_rows)(returned, places)
    mixture = lax.optimization_barrier(jnp.sum(weights[..., None] * picked.astype(jnp.float32), axis=2))
    layer_out = (shaped_hidden.astype(jnp.float32) + mixture).astype(jnp.bfloat16)

    def attend_device(items):
        return attend(items[0], w_latent, items[1], items[2], items[3])
    attention = lax.map(attend_device, (layer_out, lengths.reshape(DEVICES, R_DEV), latent_cache.reshape(DEVICES, R_DEV, L, KVL + ROPE), queries.reshape(DEVICES, R_DEV, HEADS, KVL + ROPE)))
    return (layer_out.reshape(REQUESTS, D), attention.reshape(REQUESTS, HEADS, KVL))
```

```python
import math

import jax
import jax.numpy as jnp
from jax import lax
from jax.sharding import PartitionSpec as P

KVL = 512
QK_DIM = 192
AXES = ("role", "dev")
LANES = 128


def place(yh, z, x, yl, core):
    return (((yh * 4 + z) * 4 + x) * 2 + yl) * 2 + core


def shift_pairs(core_axes, offset):
    pairs = []
    for yh in range(2):
        for z in range(4):
            for x in range(4):
                for yl in range(2):
                    for core in range(2):
                        spot = {"x": x, "y": yh * 2 + yl, "z": z}
                        axis = core_axes[core]
                        spot[axis] = (spot[axis] + offset) % 4
                        there = place(spot["y"] // 2, spot["z"], spot["x"], spot["y"] % 2, core)
                        pairs.append((there, place(yh, z, x, yl, core)))
    return pairs


AXIS = {"a": ("x", "z"), "b": ("z", "x"), "y": ("y", "y")}


def shift(values, axis, offset):
    return lax.ppermute(values, AXES, shift_pairs(AXIS[axis], offset))


def swap_cores(values):
    return lax.ppermute(values, AXES, [(d, d ^ 1) for d in range(128)])


def gather(values, axis):
    near = shift(values, axis, 1)
    back = shift(values, axis, 3)
    far = shift(values, axis, 2)
    return [values, near, far, back]


def reduce(blocks, axis):
    near = shift(blocks[1], axis, 3)
    back = shift(blocks[3], axis, 1)
    far = shift(blocks[2], axis, 2)
    f = jnp.float32
    return blocks[0].astype(f) + near.astype(f) + back.astype(f) + far.astype(f)


def normalize(values):
    return values * lax.rsqrt(jnp.mean(values * values, axis=-1, keepdims=True) + 1e-06)


def prepare(router, routes, hidden):
    experts = router.shape[1]
    normed = normalize(hidden.astype(jnp.float32)).astype(jnp.bfloat16)
    logits = jnp.dot(normed, router, preferred_element_type=jnp.float32)
    labels = jnp.arange(experts, dtype=jnp.int32)
    chosen = jnp.any(routes[:, :, None] == labels[None, None, :], axis=1)
    affinity = jnp.where(chosen, jax.nn.sigmoid(logits), 0.0)
    weights = 2.5 * affinity / jnp.sum(affinity, axis=1, keepdims=True)
    high = weights.astype(jnp.bfloat16)
    low = (weights - high.astype(jnp.float32)).astype(jnp.bfloat16)
    pad = jnp.zeros((hidden.shape[0], LANES - 2 * experts), jnp.bfloat16)
    return normed, jnp.concatenate([high, low, pad], axis=1)


def rotate(values, positions):
    half = values.shape[-1] // 2
    indices = jnp.arange(half, dtype=jnp.float32)
    inverse = jnp.exp(indices * (-2.0 * math.log(10000.0) / values.shape[-1]))
    angles = positions.astype(jnp.float32)[:, None] * inverse[None, :]
    leading = values[:, :half]
    trailing = values[:, half:]
    return jnp.concatenate(
        [
            leading * jnp.cos(angles) - trailing * jnp.sin(angles),
            leading * jnp.sin(angles) + trailing * jnp.cos(angles),
        ],
        axis=1,
    )


def attend_cache(lengths, latent_cache, queries):
    scale = 1.0 / math.sqrt(QK_DIM)
    scores = (
        jnp.einsum("rhc,rjc->rhj", queries, latent_cache, preferred_element_type=jnp.float32)
        * scale
    )
    positions = jnp.arange(latent_cache.shape[1], dtype=jnp.int32)
    valid = positions[None, None, :] < lengths[:, None, None]
    highest = jnp.max(jnp.where(valid, scores, -jnp.inf), axis=2)
    probs = jnp.where(valid, jnp.exp(scores - highest[:, :, None]), 0.0).astype(jnp.bfloat16)
    total = jnp.sum(probs.astype(jnp.float32), axis=2)
    summed = jnp.einsum(
        "rhj,rjc->rhc", probs, latent_cache[:, :, :KVL], preferred_element_type=jnp.float32
    )
    return highest, total, summed


def attend_own(layer_out, w_latent, lengths, queries, highest, total, summed):
    input_new = normalize(layer_out.astype(jnp.float32)).astype(jnp.bfloat16)
    projected = jnp.dot(input_new, w_latent, preferred_element_type=jnp.float32)
    latent_new = normalize(projected[:, :KVL]).astype(jnp.bfloat16)
    rotary_new = rotate(projected[:, KVL:], lengths).astype(jnp.bfloat16)
    key_new = jnp.concatenate([latent_new, rotary_new], axis=1)
    scale = 1.0 / math.sqrt(QK_DIM)
    own = jnp.einsum("rhc,rc->rh", queries, key_new, preferred_element_type=jnp.float32) * scale
    top = jnp.maximum(highest, own)
    fade = jnp.exp(highest - top)
    own_prob = jnp.exp(own - top)
    whole = total * fade + own_prob
    mixed = (
        summed * (fade / whole)[:, :, None]
        + (own_prob / whole)[:, :, None] * latent_new.astype(jnp.float32)[:, None, :]
    )
    return mixed.astype(jnp.bfloat16)


def body(hidden, router, routes, w_gate, w_up, w_down, w_latent, lengths, latent_cache, queries):
    bf, f32 = jnp.bfloat16, jnp.float32
    rows, width = hidden.shape
    experts = router.shape[1]
    cut = width // LANES * 2 // 3 // 2 * 2 * LANES + 2 * LANES
    cut = 38 * LANES if width == 7168 else cut
    rest = width - cut
    mine = lax.rem(lax.axis_index("dev"), experts)

    normed, gates = prepare(router, routes, hidden)
    other_gate, other_up, other_down = swap_cores(w_gate[0]), swap_cores(w_up[0]), swap_cores(w_down[0])

    first = jnp.stack(gather(normed[:, :cut], "y"))
    second = jnp.stack(gather(jnp.concatenate([normed[:, cut:], gates], axis=1), "a"))
    both = gather(jnp.concatenate([first, second], axis=2), "b")
    first = jnp.stack([block[:, :, :cut] for block in both])
    second = jnp.stack([block[:, :, cut:] for block in both])
    firsts = gather(first, "a")
    seconds = gather(second, "y")

    gates_all = jnp.stack([block[..., rest:] for block in seconds]).astype(f32)
    gates_all = gates_all[..., :experts] + gates_all[..., experts : 2 * experts]
    labels = jnp.arange(experts)
    gate_own = jnp.sum(jnp.where(labels == mine, gates_all, 0.0), axis=-1)
    gate_other = jnp.sum(jnp.where(labels == mine + 1 - 2 * (mine % 2), gates_all, 0.0), axis=-1)
    gate_own, gate_other = [
        jnp.transpose(g, (2, 1, 0, 3)).reshape(-1, 1) for g in (gate_own, gate_other)
    ]

    count = 64 * rows
    left = jnp.stack(firsts).reshape(count, cut)
    right = jnp.transpose(jnp.stack([block[..., :rest] for block in seconds]), (2, 1, 0, 3, 4))
    right = right.reshape(count, rest)

    def lift(slab):
        return jnp.dot(left, slab[:cut], preferred_element_type=f32) + jnp.dot(
            right, slab[cut:], preferred_element_type=f32
        )

    inner = jnp.concatenate(
        [
            (jax.nn.silu(lift(w_gate[0])) * lift(w_up[0]) * gate_own).astype(bf),
            (jax.nn.silu(lift(other_gate)) * lift(other_up) * gate_other).astype(bf),
        ],
        axis=1,
    )
    down = jnp.concatenate([w_down[0], other_down], axis=0)
    inner_turned = jnp.transpose(inner.reshape(4, 4, 4, rows, -1), (2, 1, 0, 3, 4)).reshape(count, -1)
    first = jnp.dot(inner, down[:, :cut], preferred_element_type=f32).astype(bf)
    second = jnp.dot(inner_turned, down[:, cut:], preferred_element_type=f32).astype(bf)

    first = reduce(first.reshape(4, 4, 4, rows, cut), "a")
    second = reduce(second.reshape(4, 4, 4, rows, rest), "y")
    both = reduce(jnp.concatenate([first, second], axis=3).astype(bf), "b").astype(bf)
    first = reduce(both[..., :cut], "y")
    second = reduce(both[..., cut:], "a")
    mixture = jnp.concatenate([first, second], axis=1)
    layer_out = (hidden.astype(f32) + mixture).astype(bf)

    highest, total, summed = attend_cache(lengths, latent_cache, queries)
    attention = attend_own(layer_out, w_latent, lengths, queries, highest, total, summed)
    return (layer_out, attention)


def solution(mesh):
    both = P(AXES)
    return jax.shard_map(
        body,
        mesh=mesh,
        in_specs=(both, P(), both, both, both, both, P(), both, both, both),
        out_specs=(both, both),
        check_vma=False,
    )
```

```python
import functools
import math

import jax
import jax.numpy as jnp
from jax import lax
from jax.experimental import pallas as pl
from jax.experimental.pallas import tpu as pltpu
from jax.sharding import PartitionSpec as P

KVL = 512
QK_DIM = 192
AXES = ("role", "dev")
LANES = 128


def place(yh, z, x, yl, core):
    return (((yh * 4 + z) * 4 + x) * 2 + yl) * 2 + core


def partners(axes, flips):
    pairs = []
    for yh in range(2):
        for z in range(4):
            for x in range(4):
                for yl in range(2):
                    for core in range(2):
                        spot = {"x": x, "y": yh * 2 + yl, "z": z}
                        spot[axes[core]] ^= flips[core]
                        there = place(spot["y"] // 2, spot["z"], spot["x"], spot["y"] % 2, core)
                        pairs.append((place(yh, z, x, yl, core), there))
    return pairs


AXIS = {"a": ("x", "z"), "b": ("z", "x"), "y": ("y", "y")}
SAME, TURNED, SPLIT = ((1, 1), (3, 3)), ((3, 3), (1, 1)), ((1, 3), (3, 1))
FAR = (2, 2)


def flip(values, axis, flips):
    return lax.ppermute(values, AXES, partners(AXIS[axis], flips))


def swap_cores(values):
    return lax.ppermute(values, AXES, [(d, d ^ 1) for d in range(128)])


def gather(values, axis, order):
    far = flip(values, axis, FAR)
    return [values, flip(values, axis, order[0]), flip(values, axis, order[1]), far]


def gather_forward(values, axis, order):
    near = flip(values, axis, order[0])
    back = flip(values, axis, order[1])
    return [values, near, back, flip(near, axis, order[1])]


def reduce(blocks, axis, order):
    f = jnp.float32
    far = flip(blocks[3], axis, FAR)
    near = flip(blocks[1], axis, order[0])
    back = flip(blocks[2], axis, order[1])
    return blocks[0].astype(f) + near.astype(f) + back.astype(f) + far.astype(f)


def reduce_forward(blocks, axis, order):
    f = jnp.float32
    far = flip(blocks[3], axis, order[1])
    back = flip(blocks[2], axis, order[1])
    near = (blocks[1].astype(f) + far.astype(f)).astype(blocks[1].dtype)
    near = flip(near, axis, order[0])
    return blocks[0].astype(f) + back.astype(f) + near.astype(f)


def normalize(values):
    return values * lax.rsqrt(jnp.mean(values * values, axis=-1, keepdims=True) + 1e-06)


def prepare(router, routes, hidden):
    experts = router.shape[1]
    normed = normalize(hidden.astype(jnp.float32)).astype(jnp.bfloat16)
    logits = jnp.dot(normed, router, preferred_element_type=jnp.float32)
    labels = jnp.arange(experts, dtype=jnp.int32)
    chosen = jnp.any(routes[:, :, None] == labels[None, None, :], axis=1)
    affinity = jnp.where(chosen, jax.nn.sigmoid(logits), 0.0)
    weights = 2.5 * affinity / jnp.sum(affinity, axis=1, keepdims=True)
    high = weights.astype(jnp.bfloat16)
    low = (weights - high.astype(jnp.float32)).astype(jnp.bfloat16)
    pad = jnp.zeros((hidden.shape[0], LANES - 2 * experts), jnp.bfloat16)
    return normed, jnp.concatenate([high, low, pad], axis=1)


def rotate(values, positions):
    half = values.shape[-1] // 2
    indices = jnp.arange(half, dtype=jnp.float32)
    inverse = jnp.exp(indices * (-2.0 * math.log(10000.0) / values.shape[-1]))
    angles = positions.astype(jnp.float32)[:, None] * inverse[None, :]
    leading = values[:, :half]
    trailing = values[:, half:]
    return jnp.concatenate(
        [
            leading * jnp.cos(angles) - trailing * jnp.sin(angles),
            leading * jnp.sin(angles) + trailing * jnp.cos(angles),
        ],
        axis=1,
    )


def attend_cache(lengths, latent_cache, queries):
    scale = 1.0 / math.sqrt(QK_DIM)
    scores = (
        jnp.einsum("rhc,rjc->rhj", queries, latent_cache, preferred_element_type=jnp.float32)
        * scale
    )
    positions = jnp.arange(latent_cache.shape[1], dtype=jnp.int32)
    valid = positions[None, None, :] < lengths[:, None, None]
    highest = jnp.max(jnp.where(valid, scores, -jnp.inf), axis=2)
    probs = jnp.where(valid, jnp.exp(scores - highest[:, :, None]), 0.0).astype(jnp.bfloat16)
    total = jnp.sum(probs.astype(jnp.float32), axis=2)
    summed = jnp.einsum(
        "rhj,rjc->rhc", probs, latent_cache[:, :, :KVL], preferred_element_type=jnp.float32
    )
    return highest, total, summed


def attend_own(layer_out, w_latent, lengths, queries, highest, total, summed):
    input_new = normalize(layer_out.astype(jnp.float32)).astype(jnp.bfloat16)
    projected = jnp.dot(input_new, w_latent, preferred_element_type=jnp.float32)
    latent_new = normalize(projected[:, :KVL]).astype(jnp.bfloat16)
    rotary_new = rotate(projected[:, KVL:], lengths).astype(jnp.bfloat16)
    key_new = jnp.concatenate([latent_new, rotary_new], axis=1)
    scale = 1.0 / math.sqrt(QK_DIM)
    own = jnp.einsum("rhc,rc->rh", queries, key_new, preferred_element_type=jnp.float32) * scale
    top = jnp.maximum(highest, own)
    fade = jnp.exp(highest - top)
    own_prob = jnp.exp(own - top)
    whole = total * fade + own_prob
    mixed = (
        summed * (fade / whole)[:, :, None]
        + (own_prob / whole)[:, :, None] * latent_new.astype(jnp.float32)[:, None, :]
    )
    return mixed.astype(jnp.bfloat16)


STEP = 512
TURN = (0, 2, 1, 3)


def lift_kernel(steps, *refs):
    x1, x2, x3, gate_cells = refs[0:4], refs[4:8], refs[8:12], refs[12:16]
    slabs, picks, straight, turned, acc, late = refs[16:20], refs[20], refs[21], refs[22], refs[23], refs[24]
    one, two, three = steps
    k = pl.program_id(0)
    f32 = jnp.float32

    def add(target, parts, fresh):
        rows = jnp.concatenate([part[...] for part in parts], axis=0)
        for i, slab in enumerate(slabs):
            cols = pl.ds(i * 256, 256)
            product = jnp.dot(rows, slab[0], preferred_element_type=f32)
            target[:, cols] = product if fresh else target[:, cols] + product

    pl.when(k == 0)(lambda: add(acc, x1, True))
    pl.when((k > 0) & (k < one))(lambda: add(acc, x1, False))
    pl.when((k >= one) & (k < one + two))(lambda: add(acc, [x2[i] for i in TURN], False))
    pl.when(k == one + two)(lambda: add(late, x3, True))
    pl.when(k > one + two)(lambda: add(late, x3, False))

    @pl.when(k == one + two + three - 1)
    def _():
        count = acc.shape[0]

        def turn(values):
            cells = values.reshape(4, 4, 4, count // 64, values.shape[-1])
            return jnp.transpose(cells, (2, 1, 0, 3, 4)).reshape(values.shape)

        cells = jnp.concatenate([cell[...] for cell in gate_cells], axis=0).astype(f32)
        for i in range(2):
            weight = turn(cells * picks[pl.ds(i, 1), :])
            weight = jnp.sum(weight, axis=1, keepdims=True)
            gated = acc[:, pl.ds(512 * i, 256)] + turn(late[:, pl.ds(512 * i, 256)])
            lifted = acc[:, pl.ds(512 * i + 256, 256)] + turn(late[:, pl.ds(512 * i + 256, 256)])
            inner = gated / (1.0 + jnp.exp(-gated)) * lifted * weight
            straight[:, pl.ds(256 * i, 256)] = inner.astype(straight.dtype)
            turned[:, pl.ds(256 * i, 256)] = turn(inner).astype(turned.dtype)


def lift(x1, x2, x3, slabs, picks):
    steps = x1[0].shape[1] // STEP, x2[0].shape[1] // STEP, (x3[0].shape[1] - LANES) // STEP
    one, two, three = steps
    part = x1[0].shape[0]
    count = 4 * part

    def clamp(start, n):
        return lambda k: (0, jnp.clip(k - start, 0, n - 1))

    cell = lambda k: (0, three * STEP // LANES)
    in_specs = (
        [pl.BlockSpec((part, STEP), clamp(0, one))] * 4
        + [pl.BlockSpec((part, STEP), clamp(one, two))] * 4
        + [pl.BlockSpec((part, STEP), clamp(one + two, three))] * 4
        + [pl.BlockSpec((part, LANES), cell)] * 4
        + [pl.BlockSpec((1, STEP, 256), lambda k: (0, k, 0))] * 4
        + [pl.BlockSpec((8, LANES), lambda k: (0, 0))]
    )
    out = pl.BlockSpec((count, 512), lambda k: (0, 0))
    return pl.pallas_call(
        functools.partial(lift_kernel, steps),
        grid=(sum(steps),),
        in_specs=in_specs,
        out_specs=[out, out],
        out_shape=[jax.ShapeDtypeStruct((count, 512), jnp.bfloat16)] * 2,
        scratch_shapes=[pltpu.VMEM((count, 1024), jnp.float32)] * 2,
        compiler_params=pltpu.CompilerParams(vmem_limit_bytes=40 << 20),
    )(*x1, *x2, *x3, *x3, *slabs, picks)


def lower_kernel(inner, own, other, *outs):
    rows = inner.shape[0] // 4
    product = jnp.dot(inner[:, :256], own[0], preferred_element_type=jnp.float32)
    product += jnp.dot(inner[:, 256:], other[0], preferred_element_type=jnp.float32)
    for i, out in enumerate(outs):
        out[...] = product[i * rows : (i + 1) * rows].astype(out.dtype)


def lower(inner, own, other, start, width):
    rows = inner.shape[0] // 4
    slab = pl.BlockSpec((1, 256, STEP), lambda n: (0, 0, n + start // STEP))
    return pl.pallas_call(
        lower_kernel,
        grid=(width // STEP,),
        in_specs=[pl.BlockSpec(inner.shape, lambda n: (0, 0)), slab, slab],
        out_specs=[pl.BlockSpec((rows, STEP), lambda n: (0, n))] * 4,
        out_shape=[jax.ShapeDtypeStruct((rows, width), jnp.bfloat16)] * 4,
        compiler_params=pltpu.CompilerParams(vmem_limit_bytes=30 << 20),
    )(inner, own, other)


def body(hidden, router, routes, w_gate, w_up, w_down, w_latent, lengths, latent_cache, queries):
    bf, f32 = jnp.bfloat16, jnp.float32
    rows, width = hidden.shape
    experts = router.shape[1]
    third = 2560
    cut = 2 * third
    rest = width - cut
    mine = lax.rem(lax.axis_index("dev"), experts)
    other = mine + 1 - 2 * lax.rem(mine, 2)

    other_gate, other_up = swap_cores(w_gate), swap_cores(w_up)
    normed, gates = prepare(router, routes, hidden)

    first = jnp.stack(gather(normed[:, :cut], "y", SPLIT))
    second = jnp.stack(gather(jnp.concatenate([normed[:, cut:], gates], axis=1), "a", SAME))
    both, other_gate, other_up = lax.optimization_barrier(
        (jnp.concatenate([first, second], axis=2), other_gate, other_up)
    )
    other_down = swap_cores(w_down)
    both = jnp.stack(gather(both, "b", SAME))
    both, other_down = lax.optimization_barrier((both, other_down))
    flat = (16 * rows, -1)
    x1 = gather_forward(both[..., :third].reshape(flat), "a", SAME)
    x2 = gather_forward(both[..., third:cut].reshape(flat), "a", TURNED)
    x3 = gather_forward(both[..., cut:].reshape(flat), "y", SPLIT)

    spots = jnp.arange(LANES)
    marks = jnp.stack([(spots == e) | (spots == e + experts) for e in (mine, other)]).astype(f32)
    picks = jnp.concatenate([marks, jnp.zeros((6, LANES), f32)])
    straight, turned = lift(x1, x2, x3, (w_gate, w_up, other_gate, other_up), picks)
    y1 = lower(straight, w_down, other_down, 0, third)
    y2 = lower(straight, w_down, other_down, third, third)
    y3 = lower(turned, w_down, other_down, cut, rest)
    y2 = [y2[i] for i in TURN]

    y1 = reduce_forward(y1, "a", SAME).astype(bf)
    y2 = reduce_forward(y2, "a", TURNED).astype(bf)
    y3 = reduce_forward(y3, "y", SPLIT).astype(bf)
    both = jnp.concatenate([y1, y2, y3], axis=1).reshape(4, 4, rows, width)
    both = reduce([both[i] for i in range(4)], "b", SAME).astype(bf)
    first, second = both[..., :cut], both[..., cut:]
    first = reduce([first[i] for i in range(4)], "y", SPLIT)
    second = reduce([second[i] for i in range(4)], "a", SAME)
    mixture = jnp.concatenate([first, second], axis=1)
    layer_out = (hidden.astype(f32) + mixture).astype(bf)

    highest, total, summed = attend_cache(lengths, latent_cache, queries)
    attention = attend_own(layer_out, w_latent, lengths, queries, highest, total, summed)
    return (layer_out, attention)


def solution(mesh):
    both = P(AXES)
    return jax.shard_map(
        body,
        mesh=mesh,
        in_specs=(both, P(), both, both, both, both, P(), both, both, both),
        out_specs=(both, both),
        check_vma=False,
    )
```

```python
import functools
import math

import jax
import jax.numpy as jnp
from jax import lax
from jax.experimental import pallas as pl
from jax.experimental.pallas import tpu as pltpu
from jax.sharding import PartitionSpec as P

KVL = 512
QK_DIM = 192
AXES = ("role", "dev")
LANES = 128


def place(yh, z, x, yl, core):
    return (((yh * 4 + z) * 4 + x) * 2 + yl) * 2 + core


def partners(axes, flips):
    pairs = []
    for yh in range(2):
        for z in range(4):
            for x in range(4):
                for yl in range(2):
                    for core in range(2):
                        spot = {"x": x, "y": yh * 2 + yl, "z": z}
                        spot[axes[core]] ^= flips[core]
                        there = place(spot["y"] // 2, spot["z"], spot["x"], spot["y"] % 2, core)
                        pairs.append((place(yh, z, x, yl, core), there))
    return pairs


AXIS = {"a": ("x", "z"), "b": ("z", "x"), "y": ("y", "y")}
SAME, TURNED, SPLIT = ((1, 1), (3, 3)), ((3, 3), (1, 1)), ((1, 3), (3, 1))
FAR = (2, 2)


def flip(values, axis, flips):
    return lax.ppermute(values, AXES, partners(AXIS[axis], flips))


def swap_cores(values):
    return lax.ppermute(values, AXES, [(d, d ^ 1) for d in range(128)])


def gather(values, axis, order):
    far = flip(values, axis, FAR)
    return [values, flip(values, axis, order[0]), flip(values, axis, order[1]), far]


def gather_pairs(values, axis, order):
    own = jnp.concatenate([values, flip(values, axis, order[0])], axis=0)
    return own, flip(own, axis, order[1])


def reduce(blocks, axis, order):
    f = jnp.float32
    far = flip(blocks[3], axis, FAR)
    near = flip(blocks[1], axis, order[0])
    back = flip(blocks[2], axis, order[1])
    return blocks[0].astype(f) + near.astype(f) + back.astype(f) + far.astype(f)


def reduce_pairs(keep, send, axis, order):
    f = jnp.float32
    total = keep.astype(f) + flip(send, axis, order[1]).astype(f)
    half = keep.shape[0] // 2
    return total[:half] + flip(total[half:].astype(keep.dtype), axis, order[0]).astype(f)


def normalize(values):
    return values * lax.rsqrt(jnp.mean(values * values, axis=-1, keepdims=True) + 1e-06)


def prepare(router, routes, hidden):
    experts = router.shape[1]
    normed = normalize(hidden.astype(jnp.float32)).astype(jnp.bfloat16)
    logits = jnp.dot(normed, router, preferred_element_type=jnp.float32)
    labels = jnp.arange(experts, dtype=jnp.int32)
    chosen = jnp.any(routes[:, :, None] == labels[None, None, :], axis=1)
    affinity = jnp.where(chosen, jax.nn.sigmoid(logits), 0.0)
    weights = 2.5 * affinity / jnp.sum(affinity, axis=1, keepdims=True)
    high = weights.astype(jnp.bfloat16)
    low = (weights - high.astype(jnp.float32)).astype(jnp.bfloat16)
    pad = jnp.zeros((hidden.shape[0], LANES - 2 * experts), jnp.bfloat16)
    return normed, jnp.concatenate([high, low, pad], axis=1)


def rotate(values, positions):
    half = values.shape[-1] // 2
    indices = jnp.arange(half, dtype=jnp.float32)
    inverse = jnp.exp(indices * (-2.0 * math.log(10000.0) / values.shape[-1]))
    angles = positions.astype(jnp.float32)[:, None] * inverse[None, :]
    leading = values[:, :half]
    trailing = values[:, half:]
    return jnp.concatenate(
        [
            leading * jnp.cos(angles) - trailing * jnp.sin(angles),
            leading * jnp.sin(angles) + trailing * jnp.cos(angles),
        ],
        axis=1,
    )


def attend_cache(lengths, latent_cache, queries):
    scale = 1.0 / math.sqrt(QK_DIM)
    scores = (
        jnp.einsum("rhc,rjc->rhj", queries, latent_cache, preferred_element_type=jnp.float32)
        * scale
    )
    positions = jnp.arange(latent_cache.shape[1], dtype=jnp.int32)
    valid = positions[None, None, :] < lengths[:, None, None]
    highest = jnp.max(jnp.where(valid, scores, -jnp.inf), axis=2)
    probs = jnp.where(valid, jnp.exp(scores - highest[:, :, None]), 0.0).astype(jnp.bfloat16)
    total = jnp.sum(probs.astype(jnp.float32), axis=2)
    summed = jnp.einsum(
        "rhj,rjc->rhc", probs, latent_cache[:, :, :KVL], preferred_element_type=jnp.float32
    )
    return highest, total, summed


def attend_own(layer_out, w_latent, lengths, queries, highest, total, summed):
    input_new = normalize(layer_out.astype(jnp.float32)).astype(jnp.bfloat16)
    projected = jnp.dot(input_new, w_latent, preferred_element_type=jnp.float32)
    latent_new = normalize(projected[:, :KVL]).astype(jnp.bfloat16)
    rotary_new = rotate(projected[:, KVL:], lengths).astype(jnp.bfloat16)
    key_new = jnp.concatenate([latent_new, rotary_new], axis=1)
    scale = 1.0 / math.sqrt(QK_DIM)
    own = jnp.einsum("rhc,rc->rh", queries, key_new, preferred_element_type=jnp.float32) * scale
    top = jnp.maximum(highest, own)
    fade = jnp.exp(highest - top)
    own_prob = jnp.exp(own - top)
    whole = total * fade + own_prob
    mixed = (
        summed * (fade / whole)[:, :, None]
        + (own_prob / whole)[:, :, None] * latent_new.astype(jnp.float32)[:, None, :]
    )
    return mixed.astype(jnp.bfloat16)


HIDDEN = 256


def copy_in(pairs, sems):
    copies = [pltpu.make_async_copy(src, dst, sems.at[i]) for i, (src, dst) in enumerate(pairs)]
    for copy in copies:
        copy.start()
    return copies


def spans(widths):
    starts = [sum(widths[:i]) for i in range(len(widths))]
    return list(zip(starts, widths))


def slab_pairs(slabs, held, widths):
    return [
        (slab.at[0, pl.ds(start, width)], held.at[i, pl.ds(start, width)])
        for start, width in spans(widths)
        for i, slab in enumerate(slabs)
    ]


def multiply(copies, held, rows, widths, store):
    for part, (start, width) in enumerate(spans(widths)):
        for i in range(4):
            copies[part * 4 + i].wait()
            store(
                part,
                i,
                jnp.dot(
                    rows[part][:, :width],
                    held[i, pl.ds(start, width)],
                    preferred_element_type=jnp.float32,
                ),
            )


def early_kernel(widths, x1, x2, x3, s1, s2, s3, s4, h1, h2, h3, held, sems):
    copies = copy_in(slab_pairs((s1, s2, s3, s4), held, widths), sems)
    outs = (h1, h2, h3)

    def store(part, i, product):
        outs[part][:, pl.ds(i * HIDDEN, HIDDEN)] = product

    multiply(copies, held, (x1, x2, x3), widths, store)


def early(rows, slabs, widths):
    count = rows[0].shape[0]
    vmem, any_ = pl.BlockSpec(memory_space=pltpu.VMEM), pl.BlockSpec(memory_space=pl.ANY)
    return pl.pallas_call(
        functools.partial(early_kernel, widths),
        in_specs=[vmem] * 3 + [any_] * 4,
        out_specs=[vmem] * 3,
        out_shape=[jax.ShapeDtypeStruct((count, 4 * HIDDEN), jnp.float32)] * 3,
        scratch_shapes=[
            pltpu.VMEM((4, sum(widths), HIDDEN), jnp.bfloat16),
            pltpu.SemaphoreType.DMA((12,)),
        ],
        compiler_params=pltpu.CompilerParams(vmem_limit_bytes=34 << 20),
    )(*rows, *slabs)


def late_kernel(widths, x1, x2, x3, h1, h2, h3, before, picks, s1, s2, s3, s4, own, other, o1, o2, o3, straight, turned, g1, g2, g3, held, low, out1, out2, out3, sems, low_sems, out_sems):
    f32, bf = jnp.float32, jnp.bfloat16
    copies = copy_in(slab_pairs((s1, s2, s3, s4), held, widths), sems)
    low_copies = copy_in(
        [
            (slab.at[0, :, pl.ds(start, width)], low.at[pl.ds(i * HIDDEN, HIDDEN), pl.ds(start, width)])
            for start, width in spans(widths)
            for i, slab in enumerate((own, other))
        ],
        low_sems,
    )
    fresh = (g1, g2, g3)

    def store(part, i, product):
        fresh[part][:, pl.ds(i * HIDDEN, HIDDEN)] = product

    multiply(copies, held, (x1, x2, x3), widths, store)
    half = x1.shape[0]
    count, block = 2 * half, half // 2

    def turn(values):
        cells = values.reshape(4, 4, 4, count // 64, values.shape[-1])
        return jnp.transpose(cells, (2, 1, 0, 3, 4)).reshape(values.shape)

    def whole(i):
        cols = pl.ds(i * HIDDEN, HIDDEN)
        first = jnp.concatenate([h1[:, cols], g1[:, cols]], axis=0)
        second = jnp.concatenate(
            [h2[:block, cols], g2[:block, cols], h2[block:, cols], g2[block:, cols]], axis=0
        )
        third = jnp.concatenate([h3[:, cols], g3[:, cols]], axis=0)
        return first + second + turn(third)

    cells = jnp.concatenate([before[...], x3[:, pl.ds(widths[2], LANES)]], axis=0).astype(f32)
    for i in range(2):
        weight = turn(cells * picks[pl.ds(i, 1), :])
        weight = jnp.sum(weight, axis=1, keepdims=True)
        gated = whole(2 * i)
        inner = gated / (1.0 + jnp.exp(-gated)) * whole(2 * i + 1) * weight
        straight[:, pl.ds(HIDDEN * i, HIDDEN)] = inner.astype(bf)
        turned[:, pl.ds(HIDDEN * i, HIDDEN)] = turn(inner).astype(bf)

    leaving = (
        straight[half:, :],
        jnp.concatenate([straight[block:half, :], straight[half + block :, :]], axis=0),
        turned[half:, :],
    )
    out_copies = []
    for part, (start, width) in enumerate(spans(widths)):
        low_copies[2 * part].wait()
        low_copies[2 * part + 1].wait()
        buffer, out = (out1, out2, out3)[part], (o1, o2, o3)[part]
        buffer[...] = jnp.dot(leaving[part], low[:, pl.ds(start, width)], preferred_element_type=f32).astype(bf)
        copy = pltpu.make_async_copy(buffer, out, out_sems.at[part])
        copy.start()
        out_copies.append(copy)
    for copy in out_copies:
        copy.wait()


def late(rows, partial, before, picks, slabs, lows, widths):
    bf, f32 = jnp.bfloat16, jnp.float32
    count = rows[0].shape[0]
    vmem, any_ = pl.BlockSpec(memory_space=pltpu.VMEM), pl.BlockSpec(memory_space=pl.ANY)
    return pl.pallas_call(
        functools.partial(late_kernel, widths),
        in_specs=[vmem] * 8 + [any_] * 6,
        out_specs=[any_] * 3 + [vmem] * 2,
        out_shape=[jax.ShapeDtypeStruct((count, width), bf) for width in widths]
        + [jax.ShapeDtypeStruct((2 * count, 2 * HIDDEN), bf)] * 2,
        scratch_shapes=[pltpu.VMEM((count, 4 * HIDDEN), f32)] * 3
        + [
            pltpu.VMEM((4, sum(widths), HIDDEN), bf),
            pltpu.VMEM((2 * HIDDEN, sum(widths)), bf),
        ]
        + [pltpu.VMEM((count, width), bf) for width in widths]
        + [
            pltpu.SemaphoreType.DMA((12,)),
            pltpu.SemaphoreType.DMA((6,)),
            pltpu.SemaphoreType.DMA((3,)),
        ],
        compiler_params=pltpu.CompilerParams(vmem_limit_bytes=52 << 20),
    )(*rows, *partial, before, picks, *slabs, *lows)


def stay_kernel(widths, straight, turned, own, other, o1, o2, o3, low, sems):
    copies = copy_in(
        [
            (slab.at[0, :, pl.ds(start, width)], low.at[pl.ds(i * HIDDEN, HIDDEN), pl.ds(start, width)])
            for start, width in spans(widths)
            for i, slab in enumerate((own, other))
        ],
        sems,
    )
    half = straight.shape[0] // 2
    block = half // 2
    staying = (
        straight[:half, :],
        jnp.concatenate([straight[:block, :], straight[half : half + block, :]], axis=0),
        turned[:half, :],
    )
    for part, (start, width) in enumerate(spans(widths)):
        copies[2 * part].wait()
        copies[2 * part + 1].wait()
        product = jnp.dot(staying[part], low[:, pl.ds(start, width)], preferred_element_type=jnp.float32)
        (o1, o2, o3)[part][...] = product.astype(jnp.bfloat16)


def stay(straight, turned, lows, widths):
    vmem, any_ = pl.BlockSpec(memory_space=pltpu.VMEM), pl.BlockSpec(memory_space=pl.ANY)
    count = straight.shape[0] // 2
    return pl.pallas_call(
        functools.partial(stay_kernel, widths),
        in_specs=[vmem] * 2 + [any_] * 2,
        out_specs=[vmem] * 3,
        out_shape=[jax.ShapeDtypeStruct((count, width), jnp.bfloat16) for width in widths],
        scratch_shapes=[
            pltpu.VMEM((2 * HIDDEN, sum(widths)), jnp.bfloat16),
            pltpu.SemaphoreType.DMA((6,)),
        ],
        compiler_params=pltpu.CompilerParams(vmem_limit_bytes=20 << 20),
    )(straight, turned, *lows)


def body(hidden, router, routes, w_gate, w_up, w_down, w_latent, lengths, latent_cache, queries):
    bf, f32 = jnp.bfloat16, jnp.float32
    rows, width = hidden.shape
    experts = router.shape[1]
    third = 2560
    cut = 2 * third
    widths = (third, third, width - cut)
    mine = lax.rem(lax.axis_index("dev"), experts)
    other = mine + 1 - 2 * lax.rem(mine, 2)

    other_gate, other_up = swap_cores(w_gate), swap_cores(w_up)
    normed, gates = prepare(router, routes, hidden)

    first = gather_pairs(normed[None, :, :cut], "y", SPLIT)
    second = gather_pairs(jnp.concatenate([normed[:, cut:], gates], axis=1)[None], "a", SAME)
    both = jnp.concatenate([jnp.concatenate(first), jnp.concatenate(second)], axis=2)
    both, other_gate, other_up = lax.optimization_barrier((both, other_gate, other_up))
    other_down = swap_cores(w_down)
    both = jnp.stack(gather(both, "b", SAME))
    both, other_down = lax.optimization_barrier((both, other_down))
    flat = (16 * rows, -1)
    x1 = gather_pairs(both[..., :third].reshape(flat), "a", SAME)
    x2 = gather_pairs(both[..., third:cut].reshape(flat), "a", TURNED)
    x3 = gather_pairs(both[..., cut:].reshape(flat), "y", SPLIT)

    spots = jnp.arange(LANES)
    marks = jnp.stack([(spots == e) | (spots == e + experts) for e in (mine, other)]).astype(f32)
    picks = jnp.concatenate([marks, jnp.zeros((6, LANES), f32)])
    slabs, lows = (w_gate, w_up, other_gate, other_up), (w_down, other_down)
    partial = early((x1[0], x2[0], x3[0]), slabs, widths)
    before = x3[0][:, widths[2] :]
    *leaving, straight, turned = late(
        (x1[1], x2[1], x3[1]), partial, before, picks, slabs, lows, widths
    )
    staying = stay(straight, turned, lows, widths)

    y1 = reduce_pairs(staying[0], leaving[0], "a", SAME).astype(bf)
    y2 = reduce_pairs(staying[1], leaving[1], "a", TURNED).astype(bf)
    y3 = reduce_pairs(staying[2], leaving[2], "y", SPLIT).astype(bf)
    both = jnp.concatenate([y1, y2, y3], axis=1).reshape(4, 4, rows, width)
    both = reduce([both[i] for i in range(4)], "b", SAME).astype(bf)
    first, second = both[..., :cut], both[..., cut:]
    first = reduce([first[i] for i in range(4)], "y", SPLIT)
    second = reduce([second[i] for i in range(4)], "a", SAME)
    mixture = jnp.concatenate([first, second], axis=1)
    layer_out = (hidden.astype(f32) + mixture).astype(bf)

    highest, total, summed = attend_cache(lengths, latent_cache, queries)
    attention = attend_own(layer_out, w_latent, lengths, queries, highest, total, summed)
    return (layer_out, attention)


def solution(mesh):
    both = P(AXES)
    return jax.shard_map(
        body,
        mesh=mesh,
        in_specs=(both, P(), both, both, both, both, P(), both, both, both),
        out_specs=(both, both),
        check_vma=False,
    )
```

```python
import functools
import math

import jax
import jax.numpy as jnp
from jax import lax
from jax.experimental import pallas as pl
from jax.experimental.pallas import tpu as pltpu
from jax.sharding import PartitionSpec as P

KVL = 512
QK_DIM = 192
AXES = ("role", "dev")
LANES = 128


def place(yh, z, x, yl, core):
    return (((yh * 4 + z) * 4 + x) * 2 + yl) * 2 + core


def partners(axes, flips):
    pairs = []
    for yh in range(2):
        for z in range(4):
            for x in range(4):
                for yl in range(2):
                    for core in range(2):
                        spot = {"x": x, "y": yh * 2 + yl, "z": z}
                        spot[axes[core]] ^= flips[core]
                        there = place(spot["y"] // 2, spot["z"], spot["x"], spot["y"] % 2, core)
                        pairs.append((place(yh, z, x, yl, core), there))
    return pairs


AXIS = {"a": ("x", "z"), "b": ("z", "x"), "y": ("y", "y")}
SAME, TURNED, SPLIT = ((1, 1), (3, 3)), ((3, 3), (1, 1)), ((1, 3), (3, 1))
FAR = (2, 2)


def flip(values, axis, flips):
    return lax.ppermute(values, AXES, partners(AXIS[axis], flips))


def swap_cores(values):
    return lax.ppermute(values, AXES, [(d, d ^ 1) for d in range(128)])


def gather(values, axis, order):
    far = flip(values, axis, FAR)
    return [values, flip(values, axis, order[0]), flip(values, axis, order[1]), far]


def gather_pairs(values, axis, order):
    own = jnp.concatenate([values, flip(values, axis, order[0])], axis=0)
    return own, flip(own, axis, order[1])


def reduce(blocks, axis, order):
    f = jnp.float32
    far = flip(blocks[3], axis, FAR)
    near = flip(blocks[1], axis, order[0])
    back = flip(blocks[2], axis, order[1])
    return blocks[0].astype(f) + near.astype(f) + back.astype(f) + far.astype(f)


def reduce_pairs(keep, send, axis, order):
    f = jnp.float32
    total = keep.astype(f) + flip(send, axis, order[1]).astype(f)
    half = keep.shape[0] // 2
    return total[:half] + flip(total[half:].astype(keep.dtype), axis, order[0]).astype(f)


def together(values):
    mark = swap_cores(values[:8, :LANES])
    return values + mark[0, 0] * 0


def normalize(values):
    return values * lax.rsqrt(jnp.mean(values * values, axis=-1, keepdims=True) + 1e-06)


def prepare(router, routes, hidden):
    experts = router.shape[1]
    normed = normalize(hidden.astype(jnp.float32)).astype(jnp.bfloat16)
    logits = jnp.dot(normed, router, preferred_element_type=jnp.float32)
    labels = jnp.arange(experts, dtype=jnp.int32)
    chosen = jnp.any(routes[:, :, None] == labels[None, None, :], axis=1)
    affinity = jnp.where(chosen, jax.nn.sigmoid(logits), 0.0)
    weights = 2.5 * affinity / jnp.sum(affinity, axis=1, keepdims=True)
    high = weights.astype(jnp.bfloat16)
    low = (weights - high.astype(jnp.float32)).astype(jnp.bfloat16)
    pad = jnp.zeros((hidden.shape[0], LANES - 2 * experts), jnp.bfloat16)
    return normed, jnp.concatenate([high, low, pad], axis=1)


def rotate(values, positions):
    half = values.shape[-1] // 2
    indices = jnp.arange(half, dtype=jnp.float32)
    inverse = jnp.exp(indices * (-2.0 * math.log(10000.0) / values.shape[-1]))
    angles = positions.astype(jnp.float32)[:, None] * inverse[None, :]
    leading = values[:, :half]
    trailing = values[:, half:]
    return jnp.concatenate(
        [
            leading * jnp.cos(angles) - trailing * jnp.sin(angles),
            leading * jnp.sin(angles) + trailing * jnp.cos(angles),
        ],
        axis=1,
    )


def attend_cache(lengths, latent_cache, queries):
    scale = 1.0 / math.sqrt(QK_DIM)
    scores = (
        jnp.einsum("rhc,rjc->rhj", queries, latent_cache, preferred_element_type=jnp.float32)
        * scale
    )
    positions = jnp.arange(latent_cache.shape[1], dtype=jnp.int32)
    valid = positions[None, None, :] < lengths[:, None, None]
    highest = jnp.max(jnp.where(valid, scores, -jnp.inf), axis=2)
    probs = jnp.where(valid, jnp.exp(scores - highest[:, :, None]), 0.0).astype(jnp.bfloat16)
    total = jnp.sum(probs.astype(jnp.float32), axis=2)
    summed = jnp.einsum(
        "rhj,rjc->rhc", probs, latent_cache[:, :, :KVL], preferred_element_type=jnp.float32
    )
    return highest, total, summed


def attend_own(layer_out, w_latent, lengths, queries, highest, total, summed):
    input_new = normalize(layer_out.astype(jnp.float32)).astype(jnp.bfloat16)
    projected = jnp.dot(input_new, w_latent, preferred_element_type=jnp.float32)
    latent_new = normalize(projected[:, :KVL]).astype(jnp.bfloat16)
    rotary_new = rotate(projected[:, KVL:], lengths).astype(jnp.bfloat16)
    key_new = jnp.concatenate([latent_new, rotary_new], axis=1)
    scale = 1.0 / math.sqrt(QK_DIM)
    own = jnp.einsum("rhc,rc->rh", queries, key_new, preferred_element_type=jnp.float32) * scale
    top = jnp.maximum(highest, own)
    fade = jnp.exp(highest - top)
    own_prob = jnp.exp(own - top)
    whole = total * fade + own_prob
    mixed = (
        summed * (fade / whole)[:, :, None]
        + (own_prob / whole)[:, :, None] * latent_new.astype(jnp.float32)[:, None, :]
    )
    return mixed.astype(jnp.bfloat16)


HIDDEN = 256


def spans(widths):
    starts = [sum(widths[:i]) for i in range(len(widths))]
    return list(zip(starts, widths))


def multiply(slabs, rows, widths, outs):
    for part, (start, width) in enumerate(spans(widths)):
        for i, slab in enumerate(slabs):
            outs[part][:, pl.ds(i * HIDDEN, HIDDEN)] = jnp.dot(
                rows[part][:, :width],
                slab[0, pl.ds(start, width)],
                preferred_element_type=jnp.float32,
            )


def call(kernel, args, out_shape, scratch_shapes=(), limit=16):
    vmem = pl.BlockSpec(memory_space=pltpu.VMEM)
    return pl.pallas_call(
        kernel,
        in_specs=[vmem] * len(args),
        out_specs=[vmem] * len(out_shape),
        out_shape=out_shape,
        scratch_shapes=scratch_shapes,
        compiler_params=pltpu.CompilerParams(vmem_limit_bytes=limit << 20),
    )(*args)


def early_kernel(widths, x1, x2, x3, s1, s2, s3, s4, h1, h2, h3):
    multiply((s1, s2, s3, s4), (x1, x2, x3), widths, (h1, h2, h3))


def early(rows, slabs, widths):
    count = rows[0].shape[0]
    out_shape = [jax.ShapeDtypeStruct((count, 4 * HIDDEN), jnp.float32)] * 3
    return call(functools.partial(early_kernel, widths), (*rows, *slabs), out_shape)


def lower(rows, own, other, start, width):
    cols = pl.ds(start, width)
    product = jnp.dot(rows[:, :HIDDEN], own[0, :, cols], preferred_element_type=jnp.float32)
    product += jnp.dot(rows[:, HIDDEN:], other[0, :, cols], preferred_element_type=jnp.float32)
    return product.astype(jnp.bfloat16)


def late_kernel(widths, x1, x2, x3, h1, h2, h3, before, picks, s1, s2, s3, s4, own, other, o1, o2, o3, straight, turned, g1, g2, g3):
    f32, bf = jnp.float32, jnp.bfloat16
    multiply((s1, s2, s3, s4), (x1, x2, x3), widths, (g1, g2, g3))
    half = x1.shape[0]
    count, block = 2 * half, half // 2

    def turn(values):
        cells = values.reshape(4, 4, 4, count // 64, values.shape[-1])
        return jnp.transpose(cells, (2, 1, 0, 3, 4)).reshape(values.shape)

    def whole(i):
        cols = pl.ds(i * HIDDEN, HIDDEN)
        first = jnp.concatenate([h1[:, cols], g1[:, cols]], axis=0)
        second = jnp.concatenate(
            [h2[:block, cols], g2[:block, cols], h2[block:, cols], g2[block:, cols]], axis=0
        )
        third = jnp.concatenate([h3[:, cols], g3[:, cols]], axis=0)
        return first + second + turn(third)

    cells = jnp.concatenate([before[...], x3[:, pl.ds(widths[2], LANES)]], axis=0).astype(f32)
    for i in range(2):
        weight = turn(cells * picks[pl.ds(i, 1), :])
        weight = jnp.sum(weight, axis=1, keepdims=True)
        gated = whole(2 * i)
        inner = gated / (1.0 + jnp.exp(-gated)) * whole(2 * i + 1) * weight
        straight[:, pl.ds(HIDDEN * i, HIDDEN)] = inner.astype(bf)
        turned[:, pl.ds(HIDDEN * i, HIDDEN)] = turn(inner).astype(bf)

    leaving = (
        straight[half:, :],
        jnp.concatenate([straight[block:half, :], straight[half + block :, :]], axis=0),
        turned[half:, :],
    )
    for part, (start, width) in enumerate(spans(widths)):
        (o1, o2, o3)[part][...] = lower(leaving[part], own, other, start, width)


def late(rows, partial, before, picks, slabs, lows, widths):
    bf, f32 = jnp.bfloat16, jnp.float32
    count = rows[0].shape[0]
    return call(
        functools.partial(late_kernel, widths),
        (*rows, *partial, before, picks, *slabs, *lows),
        [jax.ShapeDtypeStruct((count, width), bf) for width in widths]
        + [jax.ShapeDtypeStruct((2 * count, 2 * HIDDEN), bf)] * 2,
        [pltpu.VMEM((count, 4 * HIDDEN), f32)] * 3,
    )


def stay_kernel(widths, straight, turned, own, other, o1, o2, o3):
    half = straight.shape[0] // 2
    block = half // 2
    staying = (
        straight[:half, :],
        jnp.concatenate([straight[:block, :], straight[half : half + block, :]], axis=0),
        turned[:half, :],
    )
    for part, (start, width) in enumerate(spans(widths)):
        (o1, o2, o3)[part][...] = lower(staying[part], own, other, start, width)


def stay(straight, turned, lows, widths):
    count = straight.shape[0] // 2
    out_shape = [jax.ShapeDtypeStruct((count, width), jnp.bfloat16) for width in widths]
    return call(functools.partial(stay_kernel, widths), (straight, turned, *lows), out_shape)


def body(hidden, router, routes, w_gate, w_up, w_down, w_latent, lengths, latent_cache, queries):
    bf, f32 = jnp.bfloat16, jnp.float32
    rows, width = hidden.shape
    experts = router.shape[1]
    third = 19 * LANES
    cut = 2 * third
    widths = (third, third, width - cut)
    mine = lax.rem(lax.axis_index("dev"), experts)
    other = mine + 1 - 2 * lax.rem(mine, 2)

    other_gate, other_up = swap_cores(w_gate), swap_cores(w_up)
    normed, gates = prepare(router, routes, hidden)

    first = gather_pairs(normed[None, :, :cut], "y", SPLIT)
    second = gather_pairs(jnp.concatenate([normed[:, cut:], gates], axis=1)[None], "a", SAME)
    both = jnp.concatenate([jnp.concatenate(first), jnp.concatenate(second)], axis=2)
    both, other_gate, other_up = lax.optimization_barrier((both, other_gate, other_up))
    other_down = swap_cores(w_down)
    both = jnp.stack(gather(both, "b", SAME))
    both, other_down = lax.optimization_barrier((both, other_down))
    flat = (16 * rows, -1)
    x1 = gather_pairs(both[..., :third].reshape(flat), "a", SAME)
    x2 = gather_pairs(both[..., third:cut].reshape(flat), "a", TURNED)
    x3 = gather_pairs(both[..., cut:].reshape(flat), "y", SPLIT)

    spots = jnp.arange(LANES)
    marks = jnp.stack([(spots == e) | (spots == e + experts) for e in (mine, other)]).astype(f32)
    picks = jnp.concatenate([marks, jnp.zeros((6, LANES), f32)])
    slabs, lows = (w_gate, w_up, other_gate, other_up), (w_down, other_down)
    partial = early((x1[0], x2[0], x3[0]), slabs, widths)
    before = x3[0][:, widths[2] :]
    *leaving, straight, turned = late(
        (x1[1], x2[1], x3[1]), partial, before, picks, slabs, lows, widths
    )
    staying = stay(straight, turned, lows, widths)

    y1 = reduce_pairs(staying[0], leaving[0], "a", SAME).astype(bf)
    y2 = reduce_pairs(staying[1], leaving[1], "a", TURNED).astype(bf)
    y3 = reduce_pairs(staying[2], leaving[2], "y", SPLIT).astype(bf)
    both = together(jnp.concatenate([y1, y2, y3], axis=1)).reshape(4, 4, rows, width)
    both = reduce([both[i] for i in range(4)], "b", SAME).astype(bf)
    first, second = both[..., :cut], both[..., cut:]
    first = reduce([first[i] for i in range(4)], "y", SPLIT)
    second = reduce([second[i] for i in range(4)], "a", SAME)
    mixture = jnp.concatenate([first, second], axis=1)
    layer_out = (hidden.astype(f32) + mixture).astype(bf)

    highest, total, summed = attend_cache(lengths, latent_cache, queries)
    attention = attend_own(layer_out, w_latent, lengths, queries, highest, total, summed)
    return (layer_out, attention)


def solution(mesh):
    both = P(AXES)
    return jax.shard_map(
        body,
        mesh=mesh,
        in_specs=(both, P(), both, both, both, both, P(), both, both, both),
        out_specs=(both, both),
        check_vma=False,
    )
```

```python
import functools
import math

import jax
import jax.numpy as jnp
from jax import lax
from jax.experimental import pallas as pl
from jax.experimental.pallas import tpu as pltpu
from jax.sharding import PartitionSpec as P

KVL = 512
QK_DIM = 192
AXES = ("role", "dev")
LANES = 128


def place(yh, z, x, yl, core):
    return (((yh * 4 + z) * 4 + x) * 2 + yl) * 2 + core


def partners(axes, flips):
    pairs = []
    for yh in range(2):
        for z in range(4):
            for x in range(4):
                for yl in range(2):
                    for core in range(2):
                        spot = {"x": x, "y": yh * 2 + yl, "z": z}
                        spot[axes[core]] ^= flips[core]
                        there = place(spot["y"] // 2, spot["z"], spot["x"], spot["y"] % 2, core)
                        pairs.append((place(yh, z, x, yl, core), there))
    return pairs


AXIS = {"a": ("x", "z"), "b": ("z", "x"), "y": ("y", "y")}
SAME, TURNED, SPLIT = ((1, 1), (3, 3)), ((3, 3), (1, 1)), ((1, 3), (3, 1))
FAR = (2, 2)


def flip(values, axis, flips):
    return lax.ppermute(values, AXES, partners(AXIS[axis], flips))


def swap_cores(values):
    return lax.ppermute(values, AXES, [(d, d ^ 1) for d in range(128)])


def gather(values, axis, order):
    far = flip(values, axis, FAR)
    return [values, flip(values, axis, order[0]), flip(values, axis, order[1]), far]


def gather_pairs(values, axis, order):
    own = jnp.concatenate([values, flip(values, axis, order[0])], axis=0)
    return own, flip(own, axis, order[1])


def reduce(blocks, axis, order):
    f = jnp.float32
    far = flip(blocks[3], axis, FAR)
    near = flip(blocks[1], axis, order[0])
    back = flip(blocks[2], axis, order[1])
    return blocks[0].astype(f) + near.astype(f) + back.astype(f) + far.astype(f)


def reduce_pairs(keep, send, axis, order):
    f = jnp.float32
    total = keep.astype(f) + flip(send, axis, order[1]).astype(f)
    half = keep.shape[0] // 2
    return total[:half] + flip(total[half:].astype(keep.dtype), axis, order[0]).astype(f)


def together(values):
    mark = swap_cores(values[:8, :LANES])
    return values + mark[0, 0] * 0


def normalize(values):
    return values * lax.rsqrt(jnp.mean(values * values, axis=-1, keepdims=True) + 1e-06)


def rotate(values, positions):
    half = values.shape[-1] // 2
    indices = jnp.arange(half, dtype=jnp.float32)
    inverse = jnp.exp(indices * (-2.0 * math.log(10000.0) / values.shape[-1]))
    angles = positions.astype(jnp.float32)[:, None] * inverse[None, :]
    leading = values[:, :half]
    trailing = values[:, half:]
    return jnp.concatenate(
        [
            leading * jnp.cos(angles) - trailing * jnp.sin(angles),
            leading * jnp.sin(angles) + trailing * jnp.cos(angles),
        ],
        axis=1,
    )


def attend_cache(lengths, latent_cache, queries):
    scale = 1.0 / math.sqrt(QK_DIM)
    scores = (
        jnp.einsum("rhc,rjc->rhj", queries, latent_cache, preferred_element_type=jnp.float32)
        * scale
    )
    positions = jnp.arange(latent_cache.shape[1], dtype=jnp.int32)
    valid = positions[None, None, :] < lengths[:, None, None]
    highest = jnp.max(jnp.where(valid, scores, -jnp.inf), axis=2)
    probs = jnp.where(valid, jnp.exp(scores - highest[:, :, None]), 0.0).astype(jnp.bfloat16)
    total = jnp.sum(probs.astype(jnp.float32), axis=2)
    summed = jnp.einsum(
        "rhj,rjc->rhc", probs, latent_cache[:, :, :KVL], preferred_element_type=jnp.float32
    )
    return highest, total, summed


def attend_own(layer_out, w_latent, lengths, queries, highest, total, summed):
    input_new = normalize(layer_out.astype(jnp.float32)).astype(jnp.bfloat16)
    projected = jnp.dot(input_new, w_latent, preferred_element_type=jnp.float32)
    latent_new = normalize(projected[:, :KVL]).astype(jnp.bfloat16)
    rotary_new = rotate(projected[:, KVL:], lengths).astype(jnp.bfloat16)
    key_new = jnp.concatenate([latent_new, rotary_new], axis=1)
    scale = 1.0 / math.sqrt(QK_DIM)
    own = jnp.einsum("rhc,rc->rh", queries, key_new, preferred_element_type=jnp.float32) * scale
    top = jnp.maximum(highest, own)
    fade = jnp.exp(highest - top)
    own_prob = jnp.exp(own - top)
    whole = total * fade + own_prob
    mixed = (
        summed * (fade / whole)[:, :, None]
        + (own_prob / whole)[:, :, None] * latent_new.astype(jnp.float32)[:, None, :]
    )
    return mixed.astype(jnp.bfloat16)


HIDDEN = 256


def spans(widths):
    starts = [sum(widths[:i]) for i in range(len(widths))]
    return list(zip(starts, widths))


def call(kernel, args, in_hbm, out_shape, scratch_shapes=(), limit=16):
    vmem, hbm = pl.BlockSpec(memory_space=pltpu.VMEM), pl.BlockSpec(memory_space=pltpu.HBM)
    return pl.pallas_call(
        kernel,
        in_specs=[vmem] * (len(args) - in_hbm) + [hbm] * in_hbm,
        out_specs=[vmem] * len(out_shape),
        out_shape=out_shape,
        scratch_shapes=scratch_shapes,
        compiler_params=pltpu.CompilerParams(vmem_limit_bytes=limit << 20),
    )(*args)


def prepare_kernel(cut, hidden, router, routes, first, second):
    f32, bf = jnp.float32, jnp.bfloat16
    rows, experts = hidden.shape[0], router.shape[1]
    values = hidden[...].astype(f32)
    normed = normalize(values).astype(bf)
    first[...] = normed[:, :cut]
    rest = hidden.shape[1] - cut
    second[:, :rest] = normed[:, cut:]
    logits = jnp.dot(normed, router[...], preferred_element_type=f32)
    labels = lax.broadcasted_iota(jnp.int32, (rows, experts), 1)
    chosen = labels == routes[:, 0:1]
    for k in range(1, routes.shape[1]):
        chosen = chosen | (labels == routes[:, k : k + 1])
    affinity = jnp.where(chosen, 1.0 / (1.0 + jnp.exp(-logits)), 0.0)
    weights = 2.5 * affinity / jnp.sum(affinity, axis=1, keepdims=True)
    high = weights.astype(bf)
    low = (weights - high.astype(f32)).astype(bf)
    source = lax.broadcasted_iota(jnp.int32, (experts, LANES), 0)
    target = lax.broadcasted_iota(jnp.int32, (experts, LANES), 1)
    spread = jnp.dot(high, (source == target).astype(bf), preferred_element_type=f32)
    spread += jnp.dot(low, (source + experts == target).astype(bf), preferred_element_type=f32)
    second[:, rest:] = spread.astype(bf)


def prepare(router, routes, hidden, cut):
    rows, width = hidden.shape
    widths = (cut, width - cut + LANES)
    out_shape = [jax.ShapeDtypeStruct((rows, w), jnp.bfloat16) for w in widths]
    return call(functools.partial(prepare_kernel, cut), (hidden, router, routes), 0, out_shape)


def fetch(sources, targets, sems):
    copies = [pltpu.make_async_copy(s.at[0], t, sems.at[i]) for i, (s, t) in enumerate(zip(sources, targets))]
    for copy in copies:
        copy.start()
    return copies


def multiply(slab, i, rows, outs, widths):
    for (start, width), values, out in zip(spans(widths), rows, outs):
        out[:, pl.ds(i * HIDDEN, HIDDEN)] = jnp.dot(
            values, slab[pl.ds(start, width)], preferred_element_type=jnp.float32
        )


def lift(slabs, ring, sems, rows, outs, widths, meanwhile):
    copies = [pltpu.make_async_copy(s.at[0], ring.at[i % 2], sems.at[i]) for i, s in enumerate(slabs)]
    copies[0].start()
    copies[1].start()
    for i, copy in enumerate(copies):
        copy.wait()
        multiply(ring.at[i % 2], i, rows, outs, widths)
        if i + 2 < len(copies):
            copies[i + 2].start()
        if i == 1:
            meanwhile()


def early_kernel(widths, x1, x2, x3, s1, s2, s3, s4, h1, h2, h3, ring, sems):
    rows = [x[:, :w] for x, w in zip((x1, x2, x3), widths)]
    lift((s1, s2, s3, s4), ring, sems, rows, (h1, h2, h3), widths, lambda: None)


def early(rows, slabs, widths):
    count = rows[0].shape[0]
    return call(
        functools.partial(early_kernel, widths),
        (*rows, *slabs),
        4,
        [jax.ShapeDtypeStruct((count, 4 * HIDDEN), jnp.float32)] * 3,
        [pltpu.VMEM((2, *slabs[0].shape[1:]), jnp.bfloat16), pltpu.SemaphoreType.DMA((4,))],
        14,
    )


def late_kernel(widths, x1, x2, x3, h1, h2, h3, before, picks, s1, s2, s3, s4, own_low, low, o1, o2, o3, straight, turned, g1, g2, g3, ring, lows, sems):
    f32, bf = jnp.float32, jnp.bfloat16
    half = x1.shape[0]
    count, block = 2 * half, half // 2
    low_targets = [lows.at[pl.ds(i * HIDDEN, HIDDEN)] for i in range(2)]
    low_copies = [
        pltpu.make_async_copy(s.at[0], t, sems.at[4 + i])
        for i, (s, t) in enumerate(zip((own_low, low), low_targets))
    ]

    def fetch_lows():
        for copy in low_copies:
            copy.start()

    rows = [x[:, :w] for x, w in zip((x1, x2, x3), widths)]
    lift((s1, s2, s3, s4), ring, sems, rows, (g1, g2, g3), widths, fetch_lows)

    def turn(values):
        cells = values.reshape(4, 4, 4, count // 64, values.shape[-1])
        return jnp.transpose(cells, (2, 1, 0, 3, 4)).reshape(values.shape)

    def whole(i):
        cols = pl.ds(i * HIDDEN, HIDDEN)
        first = jnp.concatenate([h1[:, cols], g1[:, cols]], axis=0)
        second = jnp.concatenate(
            [h2[:block, cols], g2[:block, cols], h2[block:, cols], g2[block:, cols]], axis=0
        )
        third = jnp.concatenate([h3[:, cols], g3[:, cols]], axis=0)
        return first + second + turn(third)

    tile = pl.ds(widths[2], LANES)
    cells = jnp.concatenate([before[...], x3[:, tile]], axis=0).astype(f32)
    for i in range(2):
        weight = turn(cells * picks[pl.ds(i, 1), :])
        weight = jnp.sum(weight, axis=1, keepdims=True)
        gated = whole(2 * i)
        inner = gated / (1.0 + jnp.exp(-gated)) * whole(2 * i + 1) * weight
        straight[:, pl.ds(HIDDEN * i, HIDDEN)] = inner.astype(bf)
        turned[:, pl.ds(HIDDEN * i, HIDDEN)] = turn(inner).astype(bf)

    leaving = (
        straight[half:, :],
        jnp.concatenate([straight[block:half, :], straight[half + block :, :]], axis=0),
        turned[half:, :],
    )
    for copy in low_copies:
        copy.wait()
    for (start, width), values, out in zip(spans(widths), leaving, (o1, o2, o3)):
        out[...] = jnp.dot(values, lows[:, pl.ds(start, width)], preferred_element_type=f32).astype(bf)


def late(rows, partial, cells, picks, slabs, lows, widths):
    bf, f32 = jnp.bfloat16, jnp.float32
    half = rows[0].shape[0]
    depth = slabs[0].shape[1]
    return call(
        functools.partial(late_kernel, widths),
        (*rows, *partial, cells, picks, *slabs, *lows),
        6,
        [jax.ShapeDtypeStruct((half, width), bf) for width in widths]
        + [jax.ShapeDtypeStruct((2 * half, 2 * HIDDEN), bf)] * 2,
        [pltpu.VMEM((half, 4 * HIDDEN), f32)] * 3
        + [
            pltpu.VMEM((2, depth, HIDDEN), bf),
            pltpu.VMEM((2 * HIDDEN, depth), bf),
            pltpu.SemaphoreType.DMA((6,)),
        ],
        34,
    )


def stay_kernel(widths, straight, turned, own_low, low, o1, o2, o3, lows, sems):
    copies = fetch((own_low, low), [lows.at[pl.ds(i * HIDDEN, HIDDEN)] for i in range(2)], sems)
    block = straight.shape[0] // 4
    staying = (
        straight[: 2 * block, :],
        jnp.concatenate([straight[:block, :], straight[2 * block : 3 * block, :]], axis=0),
        turned[: 2 * block, :],
    )
    for copy in copies:
        copy.wait()
    for (start, width), values, out in zip(spans(widths), staying, (o1, o2, o3)):
        product = jnp.dot(values, lows[:, pl.ds(start, width)], preferred_element_type=jnp.float32)
        out[...] = product.astype(jnp.bfloat16)


def stay(straight, turned, lows, widths):
    count = straight.shape[0] // 2
    return call(
        functools.partial(stay_kernel, widths),
        (straight, turned, *lows),
        2,
        [jax.ShapeDtypeStruct((count, width), jnp.bfloat16) for width in widths],
        [pltpu.VMEM((2 * HIDDEN, lows[0].shape[2]), jnp.bfloat16), pltpu.SemaphoreType.DMA((2,))],
        14,
    )


def body(hidden, router, routes, w_gate, w_up, w_down, w_latent, lengths, latent_cache, queries):
    bf, f32 = jnp.bfloat16, jnp.float32
    rows, width = hidden.shape
    experts = router.shape[1]
    third = 19 * LANES
    cut = 2 * third
    widths = (third, third, width - cut)
    mine = lax.rem(lax.axis_index("dev"), experts)
    other = mine + 1 - 2 * lax.rem(mine, 2)

    other_gate, other_up = swap_cores(w_gate), swap_cores(w_up)
    first, second = prepare(router, routes, hidden, cut)

    first = jnp.concatenate(gather_pairs(first[None], "y", SPLIT))
    second = jnp.concatenate(gather_pairs(second[None], "a", SAME))
    both = jnp.concatenate([first, second], axis=2)
    both, other_gate, other_up = lax.optimization_barrier((both, other_gate, other_up))
    other_down = swap_cores(w_down)
    both = jnp.stack(gather(both, "b", SAME))
    both, other_down = lax.optimization_barrier((both, other_down))
    flat = (16 * rows, -1)
    x1 = gather_pairs(both[..., :third].reshape(flat), "a", SAME)
    x2 = gather_pairs(both[..., third:cut].reshape(flat), "a", TURNED)
    x3 = gather_pairs(both[..., cut:].reshape(flat), "y", SPLIT)

    spots = jnp.arange(LANES)
    marks = jnp.stack([(spots == e) | (spots == e + experts) for e in (mine, other)]).astype(f32)
    picks = jnp.concatenate([marks, jnp.zeros((6, LANES), f32)])
    slabs, lows = (w_gate, w_up, other_gate, other_up), (w_down, other_down)
    partial = early([part[0] for part in (x1, x2, x3)], slabs, widths)
    cells = x3[0][:, widths[2] :]
    last_rows = [part[1] for part in (x1, x2, x3)]
    *leaving, straight, turned = late(last_rows, partial, cells, picks, slabs, lows, widths)
    staying = stay(straight, turned, lows, widths)

    ways = (("a", SAME), ("a", TURNED), ("y", SPLIT))
    sums = [reduce_pairs(staying[i], leaving[i], *way).astype(bf) for i, way in enumerate(ways)]
    both = together(jnp.concatenate(sums, axis=1)).reshape(4, 4, rows, width)
    both = reduce([both[i] for i in range(4)], "b", SAME).astype(bf)
    first = reduce_pairs(both[:2, :, :cut], both[2:, :, :cut], "y", SPLIT)
    second = reduce_pairs(both[:2, :, cut:], both[2:, :, cut:], "a", SAME)
    mixture = jnp.concatenate([first[0], second[0]], axis=1)
    layer_out = (hidden.astype(f32) + mixture).astype(bf)

    highest, total, summed = attend_cache(lengths, latent_cache, queries)
    attention = attend_own(layer_out, w_latent, lengths, queries, highest, total, summed)
    return (layer_out, attention)


def solution(mesh):
    both = P(AXES)
    return jax.shard_map(
        body,
        mesh=mesh,
        in_specs=(both, P(), both, both, both, both, P(), both, both, both),
        out_specs=(both, both),
        check_vma=False,
    )
```

```python
import functools
import math

import jax
import jax.numpy as jnp
from jax import lax
from jax.experimental import pallas as pl
from jax.experimental.pallas import tpu as pltpu
from jax.sharding import PartitionSpec as P

KVL = 512
QK_DIM = 192
AXES = ("role", "dev")
LANES = 128


def place(yh, z, x, yl, core):
    return (((yh * 4 + z) * 4 + x) * 2 + yl) * 2 + core


def partners(axes, flips):
    pairs = []
    for yh in range(2):
        for z in range(4):
            for x in range(4):
                for yl in range(2):
                    for core in range(2):
                        spot = {"x": x, "y": yh * 2 + yl, "z": z}
                        spot[axes[core]] ^= flips[core]
                        there = place(spot["y"] // 2, spot["z"], spot["x"], spot["y"] % 2, core)
                        pairs.append((place(yh, z, x, yl, core), there))
    return pairs


AXIS = {"a": ("x", "z"), "b": ("z", "x"), "y": ("y", "y")}
SAME, TURNED, SPLIT = ((1, 1), (3, 3)), ((3, 3), (1, 1)), ((1, 3), (3, 1))
FAR = (2, 2)


def flip(values, axis, flips):
    return lax.ppermute(values, AXES, partners(AXIS[axis], flips))


def swap_cores(values):
    return lax.ppermute(values, AXES, [(d, d ^ 1) for d in range(128)])


def gather(values, axis, order):
    far = flip(values, axis, FAR)
    return [values, flip(values, axis, order[0]), flip(values, axis, order[1]), far]


def gather_pairs(values, axis, order):
    count = values.shape[0]
    room = jnp.pad(values, [(0, count)] + [(0, 0)] * (values.ndim - 1))
    room = lax.optimization_barrier(room)
    own = lax.dynamic_update_slice_in_dim(room, flip(values, axis, order[0]), count, 0)
    return own, flip(own, axis, order[1])


def reduce(blocks, axis, order):
    f = jnp.float32
    far = flip(blocks[3], axis, FAR)
    near = flip(blocks[1], axis, order[0])
    back = flip(blocks[2], axis, order[1])
    return blocks[0].astype(f) + near.astype(f) + back.astype(f) + far.astype(f)


def reduce_pairs(keep, send, axis, order):
    f = jnp.float32
    total = keep.astype(f) + flip(send, axis, order[1]).astype(f)
    half = keep.shape[0] // 2
    return total[:half] + flip(total[half:].astype(keep.dtype), axis, order[0]).astype(f)


def together(values):
    mark = swap_cores(values[:8, :LANES])
    return values + mark[0, 0] * 0


def normalize(values):
    return values * lax.rsqrt(jnp.mean(values * values, axis=-1, keepdims=True) + 1e-06)


def rotate(values, positions):
    half = values.shape[-1] // 2
    indices = jnp.arange(half, dtype=jnp.float32)
    inverse = jnp.exp(indices * (-2.0 * math.log(10000.0) / values.shape[-1]))
    angles = positions.astype(jnp.float32)[:, None] * inverse[None, :]
    leading = values[:, :half]
    trailing = values[:, half:]
    return jnp.concatenate(
        [
            leading * jnp.cos(angles) - trailing * jnp.sin(angles),
            leading * jnp.sin(angles) + trailing * jnp.cos(angles),
        ],
        axis=1,
    )


def attend_cache(lengths, latent_cache, queries):
    scale = 1.0 / math.sqrt(QK_DIM)
    scores = (
        jnp.einsum("rhc,rjc->rhj", queries, latent_cache, preferred_element_type=jnp.float32)
        * scale
    )
    positions = jnp.arange(latent_cache.shape[1], dtype=jnp.int32)
    valid = positions[None, None, :] < lengths[:, None, None]
    highest = jnp.max(jnp.where(valid, scores, -jnp.inf), axis=2)
    probs = jnp.where(valid, jnp.exp(scores - highest[:, :, None]), 0.0).astype(jnp.bfloat16)
    total = jnp.sum(probs.astype(jnp.float32), axis=2)
    summed = jnp.einsum(
        "rhj,rjc->rhc", probs, latent_cache[:, :, :KVL], preferred_element_type=jnp.float32
    )
    return highest, total, summed


def attend_own(layer_out, w_latent, lengths, queries, highest, total, summed):
    input_new = normalize(layer_out.astype(jnp.float32)).astype(jnp.bfloat16)
    projected = jnp.dot(input_new, w_latent, preferred_element_type=jnp.float32)
    latent_new = normalize(projected[:, :KVL]).astype(jnp.bfloat16)
    rotary_new = rotate(projected[:, KVL:], lengths).astype(jnp.bfloat16)
    key_new = jnp.concatenate([latent_new, rotary_new], axis=1)
    scale = 1.0 / math.sqrt(QK_DIM)
    own = jnp.einsum("rhc,rc->rh", queries, key_new, preferred_element_type=jnp.float32) * scale
    top = jnp.maximum(highest, own)
    fade = jnp.exp(highest - top)
    own_prob = jnp.exp(own - top)
    whole = total * fade + own_prob
    mixed = (
        summed * (fade / whole)[:, :, None]
        + (own_prob / whole)[:, :, None] * latent_new.astype(jnp.float32)[:, None, :]
    )
    return mixed.astype(jnp.bfloat16)


HIDDEN = 256


def spans(widths):
    starts = [sum(widths[:i]) for i in range(len(widths))]
    return list(zip(starts, widths))


def call(kernel, args, in_hbm, out_shape, scratch_shapes=(), limit=16):
    vmem, hbm = pl.BlockSpec(memory_space=pltpu.VMEM), pl.BlockSpec(memory_space=pltpu.HBM)
    return pl.pallas_call(
        kernel,
        in_specs=[vmem] * (len(args) - in_hbm) + [hbm] * in_hbm,
        out_specs=[vmem] * len(out_shape),
        out_shape=out_shape,
        scratch_shapes=scratch_shapes,
        compiler_params=pltpu.CompilerParams(vmem_limit_bytes=limit << 20),
    )(*args)


def prepare_kernel(cut, hidden, router, routes, first, second):
    f32, bf = jnp.float32, jnp.bfloat16
    rows, experts = hidden.shape[0], router.shape[1]
    values = hidden[...].astype(f32)
    normed = normalize(values).astype(bf)
    first[...] = normed[:, :cut]
    rest = hidden.shape[1] - cut
    second[:, :rest] = normed[:, cut:]
    logits = jnp.dot(normed, router[...], preferred_element_type=f32)
    labels = lax.broadcasted_iota(jnp.int32, (rows, experts), 1)
    chosen = labels == routes[:, 0:1]
    for k in range(1, routes.shape[1]):
        chosen = chosen | (labels == routes[:, k : k + 1])
    affinity = jnp.where(chosen, 1.0 / (1.0 + jnp.exp(-logits)), 0.0)
    weights = 2.5 * affinity / jnp.sum(affinity, axis=1, keepdims=True)
    high = weights.astype(bf)
    low = (weights - high.astype(f32)).astype(bf)
    source = lax.broadcasted_iota(jnp.int32, (experts, LANES), 0)
    target = lax.broadcasted_iota(jnp.int32, (experts, LANES), 1)
    spread = jnp.dot(high, (source == target).astype(bf), preferred_element_type=f32)
    spread += jnp.dot(low, (source + experts == target).astype(bf), preferred_element_type=f32)
    second[:, rest:] = spread.astype(bf)


def prepare(router, routes, hidden, cut):
    rows, width = hidden.shape
    widths = (cut, width - cut + LANES)
    out_shape = [jax.ShapeDtypeStruct((rows, w), jnp.bfloat16) for w in widths]
    return call(functools.partial(prepare_kernel, cut), (hidden, router, routes), 0, out_shape)


def fetch(sources, targets, sems):
    copies = [pltpu.make_async_copy(s.at[0], t, sems.at[i]) for i, (s, t) in enumerate(zip(sources, targets))]
    for copy in copies:
        copy.start()
    return copies


def multiply(slab, i, rows, outs, widths):
    for (start, width), values, out in zip(spans(widths), rows, outs):
        out[:, pl.ds(i * HIDDEN, HIDDEN)] = jnp.dot(
            values, slab[pl.ds(start, width)], preferred_element_type=jnp.float32
        )


def lift(slabs, ring, sems, rows, outs, widths, meanwhile):
    copies = [pltpu.make_async_copy(s.at[0], ring.at[i % 2], sems.at[i]) for i, s in enumerate(slabs)]
    copies[0].start()
    copies[1].start()
    for i, copy in enumerate(copies):
        copy.wait()
        multiply(ring.at[i % 2], i, rows, outs, widths)
        if i + 2 < len(copies):
            copies[i + 2].start()
        if i == 1:
            meanwhile()


def early_kernel(widths, x1, x2, x3, s1, s2, s3, s4, h1, h2, h3, ring, sems):
    rows = [x[:, :w] for x, w in zip((x1, x2, x3), widths)]
    lift((s1, s2, s3, s4), ring, sems, rows, (h1, h2, h3), widths, lambda: None)


def early(rows, slabs, widths):
    count = rows[0].shape[0]
    return call(
        functools.partial(early_kernel, widths),
        (*rows, *slabs),
        4,
        [jax.ShapeDtypeStruct((count, 4 * HIDDEN), jnp.float32)] * 3,
        [pltpu.VMEM((2, *slabs[0].shape[1:]), jnp.bfloat16), pltpu.SemaphoreType.DMA((4,))],
        14,
    )


def late_kernel(widths, x1, x2, x3, h1, h2, h3, before, picks, s1, s2, s3, s4, own_low, low, o1, o2, o3, straight, turned, g1, g2, g3, ring, lows, sems):
    f32, bf = jnp.float32, jnp.bfloat16
    half = x1.shape[0]
    count, block = 2 * half, half // 2
    low_targets = [lows.at[pl.ds(i * HIDDEN, HIDDEN)] for i in range(2)]
    low_copies = [
        pltpu.make_async_copy(s.at[0], t, sems.at[4 + i])
        for i, (s, t) in enumerate(zip((own_low, low), low_targets))
    ]

    def fetch_lows():
        for copy in low_copies:
            copy.start()

    rows = [x[:, :w] for x, w in zip((x1, x2, x3), widths)]
    lift((s1, s2, s3, s4), ring, sems, rows, (g1, g2, g3), widths, fetch_lows)

    def turn(values):
        cells = values.reshape(4, 4, 4, count // 64, values.shape[-1])
        return jnp.transpose(cells, (2, 1, 0, 3, 4)).reshape(values.shape)

    def whole(i):
        cols = pl.ds(i * HIDDEN, HIDDEN)
        first = jnp.concatenate([h1[:, cols], g1[:, cols]], axis=0)
        second = jnp.concatenate(
            [h2[:block, cols], g2[:block, cols], h2[block:, cols], g2[block:, cols]], axis=0
        )
        third = jnp.concatenate([h3[:, cols], g3[:, cols]], axis=0)
        return first + second + turn(third)

    tile = pl.ds(widths[2], LANES)
    cells = jnp.concatenate([before[...], x3[:, tile]], axis=0).astype(f32)
    for i in range(2):
        weight = turn(cells * picks[pl.ds(i, 1), :])
        weight = jnp.sum(weight, axis=1, keepdims=True)
        gated = whole(2 * i)
        inner = gated / (1.0 + jnp.exp(-gated)) * whole(2 * i + 1) * weight
        straight[:, pl.ds(HIDDEN * i, HIDDEN)] = inner.astype(bf)
        turned[:, pl.ds(HIDDEN * i, HIDDEN)] = turn(inner).astype(bf)

    leaving = (
        straight[half:, :],
        jnp.concatenate([straight[block:half, :], straight[half + block :, :]], axis=0),
        turned[half:, :],
    )
    for copy in low_copies:
        copy.wait()
    for (start, width), values, out in zip(spans(widths), leaving, (o1, o2, o3)):
        out[...] = jnp.dot(values, lows[:, pl.ds(start, width)], preferred_element_type=f32).astype(bf)


def late(rows, partial, cells, picks, slabs, lows, widths):
    bf, f32 = jnp.bfloat16, jnp.float32
    half = rows[0].shape[0]
    depth = slabs[0].shape[1]
    return call(
        functools.partial(late_kernel, widths),
        (*rows, *partial, cells, picks, *slabs, *lows),
        6,
        [jax.ShapeDtypeStruct((half, width), bf) for width in widths]
        + [jax.ShapeDtypeStruct((2 * half, 2 * HIDDEN), bf)] * 2,
        [pltpu.VMEM((half, 4 * HIDDEN), f32)] * 3
        + [
            pltpu.VMEM((2, depth, HIDDEN), bf),
            pltpu.VMEM((2 * HIDDEN, depth), bf),
            pltpu.SemaphoreType.DMA((6,)),
        ],
        34,
    )


def stay_kernel(widths, straight, turned, own_low, low, o1, o2, o3, lows, sems):
    copies = fetch((own_low, low), [lows.at[pl.ds(i * HIDDEN, HIDDEN)] for i in range(2)], sems)
    block = straight.shape[0] // 4
    staying = (
        straight[: 2 * block, :],
        jnp.concatenate([straight[:block, :], straight[2 * block : 3 * block, :]], axis=0),
        turned[: 2 * block, :],
    )
    for copy in copies:
        copy.wait()
    for (start, width), values, out in zip(spans(widths), staying, (o1, o2, o3)):
        product = jnp.dot(values, lows[:, pl.ds(start, width)], preferred_element_type=jnp.float32)
        out[...] = product.astype(jnp.bfloat16)


def stay(straight, turned, lows, widths):
    count = straight.shape[0] // 2
    return call(
        functools.partial(stay_kernel, widths),
        (straight, turned, *lows),
        2,
        [jax.ShapeDtypeStruct((count, width), jnp.bfloat16) for width in widths],
        [pltpu.VMEM((2 * HIDDEN, lows[0].shape[2]), jnp.bfloat16), pltpu.SemaphoreType.DMA((2,))],
        14,
    )


def body(hidden, router, routes, w_gate, w_up, w_down, w_latent, lengths, latent_cache, queries):
    bf, f32 = jnp.bfloat16, jnp.float32
    rows, width = hidden.shape
    experts = router.shape[1]
    third = 19 * LANES
    cut = 2 * third
    widths = (third, third, width - cut)
    mine = lax.rem(lax.axis_index("dev"), experts)
    other = mine + 1 - 2 * lax.rem(mine, 2)

    other_gate, other_up = swap_cores(w_gate), swap_cores(w_up)
    first, second = prepare(router, routes, hidden, cut)

    first = jnp.concatenate(gather_pairs(first[None], "y", SPLIT))
    second = jnp.concatenate(gather_pairs(second[None], "a", SAME))
    both = jnp.concatenate([first, second], axis=2)
    both, other_gate, other_up = lax.optimization_barrier((both, other_gate, other_up))
    other_down = swap_cores(w_down)
    both = jnp.stack(gather(both, "b", SAME))
    both, other_down = lax.optimization_barrier((both, other_down))
    flat = (16 * rows, -1)
    x1 = gather_pairs(both[..., :third].reshape(flat), "a", SAME)
    x2 = gather_pairs(both[..., third:cut].reshape(flat), "a", TURNED)
    x3 = gather_pairs(both[..., cut:].reshape(flat), "y", SPLIT)

    spots = jnp.arange(LANES)
    marks = jnp.stack([(spots == e) | (spots == e + experts) for e in (mine, other)]).astype(f32)
    picks = jnp.concatenate([marks, jnp.zeros((6, LANES), f32)])
    slabs, lows = (w_gate, w_up, other_gate, other_up), (w_down, other_down)
    partial = early([part[0] for part in (x1, x2, x3)], slabs, widths)
    cells = x3[0][:, widths[2] :]
    last_rows = [part[1] for part in (x1, x2, x3)]
    *leaving, straight, turned = late(last_rows, partial, cells, picks, slabs, lows, widths)
    staying = stay(straight, turned, lows, widths)

    ways = (("a", SAME), ("a", TURNED), ("y", SPLIT))
    sums = [reduce_pairs(staying[i], leaving[i], *way).astype(bf) for i, way in enumerate(ways)]
    both = together(jnp.concatenate(sums, axis=1)).reshape(4, 4, rows, width)
    both = reduce([both[i] for i in range(4)], "b", SAME).astype(bf)
    first = reduce_pairs(both[:2, :, :cut], both[2:, :, :cut], "y", SPLIT)
    second = reduce_pairs(both[:2, :, cut:], both[2:, :, cut:], "a", SAME)
    mixture = jnp.concatenate([first[0], second[0]], axis=1)
    layer_out = (hidden.astype(f32) + mixture).astype(bf)

    highest, total, summed = lax.optimization_barrier(
        attend_cache(lengths, latent_cache, queries)
    )
    attention = attend_own(layer_out, w_latent, lengths, queries, highest, total, summed)
    return (layer_out, attention)


def solution(mesh):
    both = P(AXES)
    return jax.shard_map(
        body,
        mesh=mesh,
        in_specs=(both, P(), both, both, both, both, P(), both, both, both),
        out_specs=(both, both),
        check_vma=False,
    )
```

```python
import functools
import math

import jax
import jax.numpy as jnp
from jax import lax
from jax.experimental import pallas as pl
from jax.experimental.pallas import tpu as pltpu
from jax.sharding import PartitionSpec as P

KVL = 512
QK_DIM = 192
AXES = ("role", "dev")
LANES = 128


def place(yh, z, x, yl, core):
    return (((yh * 4 + z) * 4 + x) * 2 + yl) * 2 + core


def partners(axes, flips):
    pairs = []
    for yh in range(2):
        for z in range(4):
            for x in range(4):
                for yl in range(2):
                    for core in range(2):
                        spot = {"x": x, "y": yh * 2 + yl, "z": z}
                        spot[axes[core]] ^= flips[core]
                        there = place(spot["y"] // 2, spot["z"], spot["x"], spot["y"] % 2, core)
                        pairs.append((place(yh, z, x, yl, core), there))
    return pairs


AXIS = {"a": ("x", "z"), "b": ("z", "x"), "y": ("y", "y")}
SAME, TURNED, SPLIT = ((1, 1), (3, 3)), ((3, 3), (1, 1)), ((1, 3), (3, 1))
FAR = (2, 2)


def flip(values, axis, flips):
    return lax.ppermute(values, AXES, partners(AXIS[axis], flips))


def swap_cores(values):
    return lax.ppermute(values, AXES, [(d, d ^ 1) for d in range(128)])


def gather(values, axis, order):
    far = flip(values, axis, FAR)
    return [values, flip(values, axis, order[0]), flip(values, axis, order[1]), far]


def gather_pairs(values, axis, order):
    count = values.shape[0]
    room = jnp.pad(values, [(0, count)] + [(0, 0)] * (values.ndim - 1))
    room = lax.optimization_barrier(room)
    own = lax.dynamic_update_slice_in_dim(room, flip(values, axis, order[0]), count, 0)
    return own, flip(own, axis, order[1])


def reduce(blocks, axis, order):
    f = jnp.float32
    far = flip(blocks[3], axis, FAR)
    near = flip(blocks[1], axis, order[0])
    back = flip(blocks[2], axis, order[1])
    return blocks[0].astype(f) + near.astype(f) + back.astype(f) + far.astype(f)


def reduce_pairs(keep, send, axis, order):
    f = jnp.float32
    total = keep.astype(f) + flip(send, axis, order[1]).astype(f)
    half = keep.shape[0] // 2
    return total[:half] + flip(total[half:].astype(keep.dtype), axis, order[0]).astype(f)


def together(values):
    mark = swap_cores(values[:8, :LANES])
    return values + mark[0, 0] * 0


def normalize(values):
    return values * lax.rsqrt(jnp.mean(values * values, axis=-1, keepdims=True) + 1e-06)


def rotate(values, positions):
    half = values.shape[-1] // 2
    indices = jnp.arange(half, dtype=jnp.float32)
    inverse = jnp.exp(indices * (-2.0 * math.log(10000.0) / values.shape[-1]))
    angles = positions.astype(jnp.float32)[:, None] * inverse[None, :]
    leading = values[:, :half]
    trailing = values[:, half:]
    return jnp.concatenate(
        [
            leading * jnp.cos(angles) - trailing * jnp.sin(angles),
            leading * jnp.sin(angles) + trailing * jnp.cos(angles),
        ],
        axis=1,
    )


def attend_cache(lengths, latent_cache, queries):
    scale = 1.0 / math.sqrt(QK_DIM)
    scores = (
        jnp.einsum("rhc,rjc->rhj", queries, latent_cache, preferred_element_type=jnp.float32)
        * scale
    )
    positions = jnp.arange(latent_cache.shape[1], dtype=jnp.int32)
    valid = positions[None, None, :] < lengths[:, None, None]
    highest = jnp.max(jnp.where(valid, scores, -jnp.inf), axis=2)
    probs = jnp.where(valid, jnp.exp(scores - highest[:, :, None]), 0.0).astype(jnp.bfloat16)
    total = jnp.sum(probs.astype(jnp.float32), axis=2)
    summed = jnp.einsum(
        "rhj,rjc->rhc", probs, latent_cache[:, :, :KVL], preferred_element_type=jnp.float32
    )
    return highest, total, summed


def attend_own(layer_out, w_latent, lengths, queries, highest, total, summed):
    input_new = normalize(layer_out.astype(jnp.float32)).astype(jnp.bfloat16)
    projected = jnp.dot(input_new, w_latent, preferred_element_type=jnp.float32)
    latent_new = normalize(projected[:, :KVL]).astype(jnp.bfloat16)
    rotary_new = rotate(projected[:, KVL:], lengths).astype(jnp.bfloat16)
    key_new = jnp.concatenate([latent_new, rotary_new], axis=1)
    scale = 1.0 / math.sqrt(QK_DIM)
    own = jnp.einsum("rhc,rc->rh", queries, key_new, preferred_element_type=jnp.float32) * scale
    top = jnp.maximum(highest, own)
    fade = jnp.exp(highest - top)
    own_prob = jnp.exp(own - top)
    whole = total * fade + own_prob
    mixed = (
        summed * (fade / whole)[:, :, None]
        + (own_prob / whole)[:, :, None] * latent_new.astype(jnp.float32)[:, None, :]
    )
    return mixed.astype(jnp.bfloat16)


HIDDEN = 256


def spans(widths):
    starts = [sum(widths[:i]) for i in range(len(widths))]
    return list(zip(starts, widths))


def call(kernel, args, in_hbm, out_shape, scratch_shapes=(), limit=16):
    vmem, hbm = pl.BlockSpec(memory_space=pltpu.VMEM), pl.BlockSpec(memory_space=pltpu.HBM)
    return pl.pallas_call(
        kernel,
        in_specs=[vmem] * (len(args) - in_hbm) + [hbm] * in_hbm,
        out_specs=[vmem] * len(out_shape),
        out_shape=out_shape,
        scratch_shapes=scratch_shapes,
        compiler_params=pltpu.CompilerParams(vmem_limit_bytes=limit << 20),
    )(*args)


def prepare_kernel(cut, hidden, router, routes, first, second):
    f32, bf = jnp.float32, jnp.bfloat16
    rows, experts = hidden.shape[0], router.shape[1]
    values = hidden[...].astype(f32)
    normed = normalize(values).astype(bf)
    first[...] = normed[:, :cut]
    rest = hidden.shape[1] - cut
    second[:, :rest] = normed[:, cut:]
    logits = jnp.dot(normed, router[...], preferred_element_type=f32)
    labels = lax.broadcasted_iota(jnp.int32, (rows, experts), 1)
    chosen = labels == routes[:, 0:1]
    for k in range(1, routes.shape[1]):
        chosen = chosen | (labels == routes[:, k : k + 1])
    affinity = jnp.where(chosen, 1.0 / (1.0 + jnp.exp(-logits)), 0.0)
    weights = 2.5 * affinity / jnp.sum(affinity, axis=1, keepdims=True)
    high = weights.astype(bf)
    low = (weights - high.astype(f32)).astype(bf)
    source = lax.broadcasted_iota(jnp.int32, (experts, LANES), 0)
    target = lax.broadcasted_iota(jnp.int32, (experts, LANES), 1)
    spread = jnp.dot(high, (source == target).astype(bf), preferred_element_type=f32)
    spread += jnp.dot(low, (source + experts == target).astype(bf), preferred_element_type=f32)
    second[:, rest:] = spread.astype(bf)


def prepare(router, routes, hidden, cut):
    rows, width = hidden.shape
    widths = (cut, width - cut + LANES)
    out_shape = [jax.ShapeDtypeStruct((rows, w), jnp.bfloat16) for w in widths]
    return call(functools.partial(prepare_kernel, cut), (hidden, router, routes), 0, out_shape)


def fetch(sources, targets, sems):
    copies = [pltpu.make_async_copy(s.at[0], t, sems.at[i]) for i, (s, t) in enumerate(zip(sources, targets))]
    for copy in copies:
        copy.start()
    return copies


def multiply(slab, i, rows, outs, widths):
    for (start, width), values, out in zip(spans(widths), rows, outs):
        out[:, pl.ds(i * HIDDEN, HIDDEN)] = jnp.dot(
            values, slab[pl.ds(start, width)], preferred_element_type=jnp.float32
        )


def lift(slabs, ring, sems, rows, outs, widths, meanwhile):
    copies = [pltpu.make_async_copy(s.at[0], ring.at[i % 2], sems.at[i]) for i, s in enumerate(slabs)]
    copies[0].start()
    copies[1].start()
    for i, copy in enumerate(copies):
        copy.wait()
        multiply(ring.at[i % 2], i, rows, outs, widths)
        if i + 2 < len(copies):
            copies[i + 2].start()
        if i == 1:
            meanwhile()


def early_kernel(widths, x1, x2, x3, s1, s2, s3, s4, h1, h2, h3, ring, sems):
    rows = [x[:, :w] for x, w in zip((x1, x2, x3), widths)]
    lift((s1, s2, s3, s4), ring, sems, rows, (h1, h2, h3), widths, lambda: None)


def early(rows, slabs, widths):
    count = rows[0].shape[0]
    return call(
        functools.partial(early_kernel, widths),
        (*rows, *slabs),
        4,
        [jax.ShapeDtypeStruct((count, 4 * HIDDEN), jnp.float32)] * 3,
        [pltpu.VMEM((2, *slabs[0].shape[1:]), jnp.bfloat16), pltpu.SemaphoreType.DMA((4,))],
        14,
    )


def late_kernel(widths, x1, x2, x3, h1, h2, h3, before, picks, s1, s2, s3, s4, own_low, low, o1, o2, o3, straight, turned, g1, g2, g3, ring, lows, sems):
    f32, bf = jnp.float32, jnp.bfloat16
    half = x1.shape[0]
    count, block = 2 * half, half // 2
    low_targets = [lows.at[pl.ds(i * HIDDEN, HIDDEN)] for i in range(2)]
    low_copies = [
        pltpu.make_async_copy(s.at[0], t, sems.at[4 + i])
        for i, (s, t) in enumerate(zip((own_low, low), low_targets))
    ]

    def fetch_lows():
        for copy in low_copies:
            copy.start()

    rows = [x[:, :w] for x, w in zip((x1, x2, x3), widths)]
    lift((s1, s2, s3, s4), ring, sems, rows, (g1, g2, g3), widths, fetch_lows)

    def turn(values):
        cells = values.reshape(4, 4, 4, count // 64, values.shape[-1])
        return jnp.transpose(cells, (2, 1, 0, 3, 4)).reshape(values.shape)

    def whole(i):
        cols = pl.ds(i * HIDDEN, HIDDEN)
        first = jnp.concatenate([h1[:, cols], g1[:, cols]], axis=0)
        second = jnp.concatenate(
            [h2[:block, cols], g2[:block, cols], h2[block:, cols], g2[block:, cols]], axis=0
        )
        third = jnp.concatenate([h3[:, cols], g3[:, cols]], axis=0)
        return first + second + turn(third)

    tile = pl.ds(widths[2], LANES)
    cells = jnp.concatenate([before[...], x3[:, tile]], axis=0).astype(f32)
    for i in range(2):
        weight = turn(cells * picks[pl.ds(i, 1), :])
        weight = jnp.sum(weight, axis=1, keepdims=True)
        gated = whole(2 * i)
        inner = gated / (1.0 + jnp.exp(-gated)) * whole(2 * i + 1) * weight
        straight[:, pl.ds(HIDDEN * i, HIDDEN)] = inner.astype(bf)
        turned[:, pl.ds(HIDDEN * i, HIDDEN)] = turn(inner).astype(bf)

    leaving = (
        straight[half:, :],
        jnp.concatenate([straight[block:half, :], straight[half + block :, :]], axis=0),
        turned[half:, :],
    )
    for copy in low_copies:
        copy.wait()
    for (start, width), values, out in zip(spans(widths), leaving, (o1, o2, o3)):
        out[...] = jnp.dot(values, lows[:, pl.ds(start, width)], preferred_element_type=f32).astype(bf)


def late(rows, partial, cells, picks, slabs, lows, widths):
    bf, f32 = jnp.bfloat16, jnp.float32
    half = rows[0].shape[0]
    depth = slabs[0].shape[1]
    return call(
        functools.partial(late_kernel, widths),
        (*rows, *partial, cells, picks, *slabs, *lows),
        6,
        [jax.ShapeDtypeStruct((half, width), bf) for width in widths]
        + [jax.ShapeDtypeStruct((2 * half, 2 * HIDDEN), bf)] * 2,
        [pltpu.VMEM((half, 4 * HIDDEN), f32)] * 3
        + [
            pltpu.VMEM((2, depth, HIDDEN), bf),
            pltpu.VMEM((2 * HIDDEN, depth), bf),
            pltpu.SemaphoreType.DMA((6,)),
        ],
        34,
    )


def stay_kernel(widths, straight, turned, own_low, low, o1, o2, o3, lows, sems):
    copies = fetch((own_low, low), [lows.at[pl.ds(i * HIDDEN, HIDDEN)] for i in range(2)], sems)
    block = straight.shape[0] // 4
    staying = (
        straight[: 2 * block, :],
        jnp.concatenate([straight[:block, :], straight[2 * block : 3 * block, :]], axis=0),
        turned[: 2 * block, :],
    )
    for copy in copies:
        copy.wait()
    for (start, width), values, out in zip(spans(widths), staying, (o1, o2, o3)):
        product = jnp.dot(values, lows[:, pl.ds(start, width)], preferred_element_type=jnp.float32)
        out[...] = product.astype(jnp.bfloat16)


def stay(straight, turned, lows, widths):
    count = straight.shape[0] // 2
    return call(
        functools.partial(stay_kernel, widths),
        (straight, turned, *lows),
        2,
        [jax.ShapeDtypeStruct((count, width), jnp.bfloat16) for width in widths],
        [pltpu.VMEM((2 * HIDDEN, lows[0].shape[2]), jnp.bfloat16), pltpu.SemaphoreType.DMA((2,))],
        14,
    )


def body(hidden, router, routes, w_gate, w_up, w_down, w_latent, lengths, latent_cache, queries):
    bf, f32 = jnp.bfloat16, jnp.float32
    rows, width = hidden.shape
    experts = router.shape[1]
    third = 19 * LANES
    cut = 2 * third
    widths = (third, third, width - cut)
    mine = lax.rem(lax.axis_index("dev"), experts)
    other = mine + 1 - 2 * lax.rem(mine, 2)

    other_gate, other_up = swap_cores(w_gate), swap_cores(w_up)
    first, second = prepare(router, routes, hidden, cut)

    first = jnp.concatenate(gather_pairs(first[None], "y", SPLIT))
    second = jnp.concatenate(gather_pairs(second[None], "a", SAME))
    both = jnp.concatenate([first, second], axis=2)
    both, other_gate, other_up = lax.optimization_barrier((both, other_gate, other_up))
    other_down = swap_cores(w_down)
    both = jnp.stack(gather(both, "b", SAME))
    both, other_down = lax.optimization_barrier((both, other_down))
    flat = (16 * rows, -1)
    x1 = gather_pairs(both[..., :third].reshape(flat), "a", SAME)
    x2 = gather_pairs(both[..., third:cut].reshape(flat), "a", TURNED)
    x3 = gather_pairs(both[..., cut:].reshape(flat), "y", SPLIT)

    spots = jnp.arange(LANES)
    marks = jnp.stack([(spots == e) | (spots == e + experts) for e in (mine, other)]).astype(f32)
    picks = jnp.concatenate([marks, jnp.zeros((6, LANES), f32)])
    slabs, lows = (w_gate, w_up, other_gate, other_up), (w_down, other_down)
    partial = early([part[0] for part in (x1, x2, x3)], slabs, widths)
    cells = x3[0][:, widths[2] :]
    last_rows = [part[1] for part in (x1, x2, x3)]
    *leaving, straight, turned = late(last_rows, partial, cells, picks, slabs, lows, widths)
    staying = stay(straight, turned, lows, widths)

    ways = (("a", SAME), ("a", TURNED), ("y", SPLIT))
    sums = [reduce_pairs(staying[i], leaving[i], *way).astype(bf) for i, way in enumerate(ways)]
    both = together(jnp.concatenate(sums, axis=1)).reshape(4, 4, rows, width)
    both = reduce([both[i] for i in range(4)], "b", SAME).astype(bf)
    first = reduce([both[i : i + 1, :, :cut] for i in range(4)], "y", SPLIT)
    second = reduce_pairs(both[:2, :, cut:], both[2:, :, cut:], "a", SAME)
    mixture = jnp.concatenate([first[0], second[0]], axis=1)
    layer_out = (hidden.astype(f32) + mixture).astype(bf)

    highest, total, summed = lax.optimization_barrier(
        attend_cache(lengths, latent_cache, queries)
    )
    attention = attend_own(layer_out, w_latent, lengths, queries, highest, total, summed)
    return (layer_out, attention)


def solution(mesh):
    both = P(AXES)
    return jax.shard_map(
        body,
        mesh=mesh,
        in_specs=(both, P(), both, both, both, both, P(), both, both, both),
        out_specs=(both, both),
        check_vma=False,
    )
```
